256 devices in a mesh: fsdp: 64 (over x, z, core), dp: 4 (over y).
Axes of the slice: x: 4, y: 4, z: 8, core: 2. Of those that a mesh axis runs over, the one named last changes fastest.
Arguments:
- tokens: bfloat16 [512, 7168], P(('fsdp', 'dp')), may hold values from -6 to 6
- grad_out: bfloat16 [512, 7168], P(('fsdp', 'dp')), may hold values from -1.5 to 1.5
- gate_codes: bfloat16 [7168, 16384], P('dp', 'fsdp'), may hold values from -4 to 4
- gate_scales: bfloat16 [56, 128], P('dp', 'fsdp'), may hold values from 0.003540039 to 0.03540039
- up_codes: bfloat16 [7168, 16384], P('dp', 'fsdp'), may hold values from -4 to 4
- up_scales: bfloat16 [56, 128], P('dp', 'fsdp'), may hold values from 0.003540039 to 0.03540039
- down_codes: bfloat16 [16384, 7168], P('fsdp', 'dp'), may hold values from -4 to 4
- down_scales: bfloat16 [128, 56], P('fsdp', 'dp'), may hold values from 0.0023345947 to 0.0234375
- gate_enter: bfloat16 [7168, 64], replicated, may hold values from -0.0625 to 0.0625
- gate_leave: bfloat16 [64, 16384], P(None, 'fsdp'), may hold values from -0.375 to 0.375
- up_enter: bfloat16 [7168, 64], replicated, may hold values from -0.0625 to 0.0625
- up_leave: bfloat16 [64, 16384], P(None, 'fsdp'), may hold values from -0.375 to 0.375
- down_enter: bfloat16 [16384, 64], P('fsdp'), may hold values from -0.046875 to 0.046875
- down_leave: bfloat16 [64, 7168], replicated, may hold values from -0.375 to 0.375
Outputs:
- layer_out: bfloat16 [512, 7168], P(('fsdp', 'dp'))
- grad_tokens: bfloat16 [512, 7168], P(('fsdp', 'dp'))
- d_gate_enter: float32 [7168, 64], P('fsdp')
- d_gate_leave: float32 [64, 16384], P(None, 'fsdp')
- d_up_enter: float32 [7168, 64], P('fsdp')
- d_up_leave: float32 [64, 16384], P(None, 'fsdp')
- d_down_enter: float32 [16384, 64], P('fsdp')
- d_down_leave: float32 [64, 7168], P(None, 'fsdp')
The draws below stay inside these ranges and needn't reach their ends.
All inputs are finite; a program needn't handle non-finite values.
Results may differ from the reference program's by a relative error of at most 0.015.
Values may be sent and summed in bfloat16 or wider, within the bound.
A program may use at most 128 MiB of HBM per device.

```python
import math
import jax
import jax.numpy as jnp

D = 7168
FF = 16384
R = 64
BLOCK = 128
TOKENS = 512


def steps_of(stream_key, shape, shards, least, largest):
    def one(dim, blocks):
        steps = jax.random.uniform(jax.random.fold_in(jax.random.fold_in(stream_key, 6), dim), (blocks,), jnp.float32, least / len(shards), largest / len(shards))
        return jnp.repeat(jnp.exp(steps), shape[dim] // blocks).reshape((-1,) + (1,) * (len(shape) - dim - 1))

    factor_of = one(*shards[0])
    for cut in shards[1:]:
        factor_of = factor_of * one(*cut)
    return factor_of


def centred(own_key, dims, deviation, limit, cuts=(), dtype=jnp.bfloat16):
    result = jax.random.normal(own_key, dims, jnp.float32) * deviation
    if len(cuts) > 0:
        result = steps_of(own_key, dims, cuts, -0.22, 0.18) * result
    return jnp.clip(result, min=-limit, max=limit).astype(dtype)


def setup_inputs(seed: int = 0) -> dict:
    seeds = jax.random.split(jax.random.key(seed), 15)
    return {
        "tokens": centred(seeds[0], (TOKENS, D), 1.0, 6.0, ((0, 256),)),
        "grad_out": centred(seeds[1], (TOKENS, D), 0.25, 1.5, ((0, 256),)),
        "gate_codes": centred(seeds[2], (D, FF), 1.0, 4.0, ((0, 4), (1, 64))),
        "gate_scales": jnp.clip(jnp.exp(math.log(0.03540039) - 2.3025851 * jax.random.uniform(seeds[3], (D // BLOCK, FF // BLOCK), jnp.float32) ** steps_of(seeds[3], (D // BLOCK, FF // BLOCK), ((0, 4), (1, 64)), -0.2, 0.2)), 0.003540039, 0.03540039).astype(jnp.bfloat16),
        "up_codes": centred(seeds[4], (D, FF), 1.0, 4.0, ((0, 4), (1, 64))),
        "up_scales": jnp.clip(jnp.exp(math.log(0.03540039) - 2.3025851 * jax.random.uniform(seeds[5], (D // BLOCK, FF // BLOCK), jnp.float32) ** steps_of(seeds[5], (D // BLOCK, FF // BLOCK), ((0, 4), (1, 64)), -0.2, 0.2)), 0.003540039, 0.03540039).astype(jnp.bfloat16),
        "down_codes": centred(seeds[6], (FF, D), 1.0, 4.0, ((0, 64), (1, 4))),
        "down_scales": jnp.clip(jnp.exp(math.log(0.0234375) - 2.306499 * jax.random.uniform(seeds[7], (FF // BLOCK, D // BLOCK), jnp.float32) ** steps_of(seeds[7], (FF // BLOCK, D // BLOCK), ((0, 64), (1, 4)), -0.2, 0.2)), 0.0023345947, 0.0234375).astype(jnp.bfloat16),
        "gate_enter": centred(seeds[8], (D, R), D ** -0.5, 0.0625),
        "gate_leave": centred(seeds[9], (R, FF), (4 * R) ** -0.5, 0.375, ((1, 64),)),
        "up_enter": centred(seeds[10], (D, R), D ** -0.5, 0.0625),
        "up_leave": centred(seeds[11], (R, FF), (4 * R) ** -0.5, 0.375, ((1, 64),)),
        "down_enter": centred(seeds[12], (FF, R), FF ** -0.5, 0.046875, ((0, 64),)),
        "down_leave": centred(seeds[13], (R, D), (4 * R) ** -0.5, 0.375),
    }


def dequant(codes, scales):
    rows, cols = codes.shape
    tiles = codes.astype(jnp.float32).reshape(rows // BLOCK, BLOCK, cols // BLOCK, BLOCK)
    tiles = tiles * scales.astype(jnp.float32)[:, None, :, None]
    return tiles.reshape(rows, cols).astype(jnp.bfloat16)


def mult(a, b):
    return jnp.dot(a, b, preferred_element_type=jnp.float32)


def reference(tokens, grad_out, gate_codes, gate_scales, up_codes, up_scales, down_codes, down_scales, gate_enter, gate_leave, up_enter, up_leave, down_enter, down_leave):
    gate_weight = dequant(gate_codes, gate_scales)
    up_weight = dequant(up_codes, up_scales)
    down_weight = dequant(down_codes, down_scales)
    gate_in = mult(tokens, gate_enter).astype(jnp.bfloat16)
    up_in = mult(tokens, up_enter).astype(jnp.bfloat16)
    gate = mult(tokens, gate_weight) + mult(gate_in, gate_leave)
    up = mult(tokens, up_weight) + mult(up_in, up_leave)
    sigma = jax.nn.sigmoid(gate)
    active = gate * sigma
    hidden = (active * up).astype(jnp.bfloat16)
    down_mid = mult(hidden, down_enter).astype(jnp.bfloat16)
    layer_out = (mult(hidden, down_weight) + mult(down_mid, down_leave)).astype(jnp.bfloat16)
    back_mid = mult(grad_out, down_leave.T).astype(jnp.bfloat16)
    grad_hidden = mult(grad_out, down_weight.T) + mult(back_mid, down_enter.T)
    grad_gate = (grad_hidden * up * sigma * (1.0 + gate * (1.0 - sigma))).astype(jnp.bfloat16)
    grad_up = (grad_hidden * active).astype(jnp.bfloat16)
    gate_back = mult(grad_gate, gate_leave.T).astype(jnp.bfloat16)
    up_back = mult(grad_up, up_leave.T).astype(jnp.bfloat16)
    grad_tokens = (mult(grad_gate, gate_weight.T) + mult(grad_up, up_weight.T)
                   + mult(gate_back, gate_enter.T) + mult(up_back, up_enter.T)).astype(jnp.bfloat16)
    d_gate_enter = mult(tokens.T, gate_back)
    d_up_enter = mult(tokens.T, up_back)
    d_gate_leave = mult(gate_in.T, grad_gate)
    d_up_leave = mult(up_in.T, grad_up)
    d_down_enter = mult(hidden.T, back_mid)
    d_down_leave = mult(down_mid.T, grad_out)
    return (layer_out, grad_tokens, d_gate_enter, d_gate_leave, d_up_enter, d_up_leave, d_down_enter, d_down_leave)
```

```python
import jax
import jax.numpy as jnp
from jax import lax
from jax.experimental import pallas as pl
from jax.experimental.pallas import tpu as pltpu
from jax.sharding import PartitionSpec as P

NX, NZ, NY = 4, 8, 4
KP, KE, EX = 1792, 1920, 128
G, H, R = 16, 256, 64
NB = 384
BF, F32 = jnp.bfloat16, jnp.float32
MESH = pl.DeviceIdType.MESH
ORDER = (0, 7, 1, 6, 2, 5, 3, 4)


def mm(a, b):
    return jnp.dot(a, b, preferred_element_type=F32)


def mm_nt(a, b):
    return lax.dot_general(a, b, (((1,), (1,)), ((), ())), preferred_element_type=F32)


def mm_tn(a, b):
    return lax.dot_general(a, b, (((0,), (0,)), ((), ())), preferred_element_type=F32)


def kernel(
    send_ref, sc_ref, gc_hbm, uc_hbm, dc_hbm, gl_ref, ul_ref, de_ref, ge_hbm, ue_hbm, dl_hbm,
    rows_out, dge_out, due_out, ddl_out, dgl_out, dul_out, dde_out,
    gcv, ucv, dcv, gev, uev, dlv, ldsem,
    st1, s1s, s1r,
    wgu, wd, wss, wsr,
    aa, ags, agx, agr,
    ext, extp, exs, exr,
    part, gus, rgu, gur,
    parth, hs, rh, hr,
    hb, hbs, hall, hallr,
    gb, gbs, gall, gallr,
    po, rss, rsss, rsr, rsrs,
    xs, xss, xr, xrs,
    msg, msgs, rowsr, rowss,
    smx, sm1, sm2, t0s, t0r, t1s, t1r,
    res, mb, fd, t3s, t3r,
    dlp, dlr, dep, der, las, lar,
):
    f = lax.axis_index("fsdp")
    y = lax.axis_index("dp")
    x = lax.div(f, 16)
    z = lax.rem(lax.div(f, 2), 8)
    c = lax.rem(f, 2)
    o = 1 - c

    def fid(xx, zz, cc):
        return xx * 16 + zz * 2 + cc

    def m4(v):
        return lax.rem(v, 4)

    def m8(v):
        return lax.rem(v, 8)

    def rcopy(src, dst, ssem, rsem, ff, yy):
        return pltpu.make_async_remote_copy(
            src_ref=src, dst_ref=dst, send_sem=ssem, recv_sem=rsem,
            device_id={"fsdp": ff, "dp": yy}, device_id_type=MESH,
        )

    def wait(ref, sem):
        pltpu.make_async_copy(ref, ref, sem).wait()

    pending = []

    def send(src, dst, ssem, rsem, ff, yy, own=None):
        if own is None:
            rcopy(src, dst, ssem, rsem, ff, yy).start()
            pending.append((src, ssem, None))
            return
        away = jnp.logical_not(own)

        @pl.when(own)
        def _():
            pltpu.make_async_copy(src, dst, rsem).start()

        @pl.when(away)
        def _():
            rcopy(src, dst, ssem, rsem, ff, yy).start()

        pending.append((src, ssem, away))

    def drain():
        for src, ssem, cond in pending:
            if cond is None:
                wait(src, ssem)
            else:
                @pl.when(cond)
                def _(src=src, ssem=ssem):
                    wait(src, ssem)
        pending.clear()

    loads = [
        pltpu.make_async_copy(gc_hbm, gcv, ldsem.at[0]),
        pltpu.make_async_copy(uc_hbm, ucv, ldsem.at[1]),
        pltpu.make_async_copy(dc_hbm, dcv, ldsem.at[2]),
        pltpu.make_async_copy(ge_hbm.at[pl.ds(y * KP, KP)], gev, ldsem.at[3]),
        pltpu.make_async_copy(ue_hbm.at[pl.ds(y * KP, KP)], uev, ldsem.at[4]),
        pltpu.make_async_copy(dl_hbm.at[:, pl.ds(pl.multiple_of(y * KP, 128), KP)], dlv, ldsem.at[5]),
    ]
    for ld in loads:
        ld.start()

    barrier = pltpu.get_barrier_semaphore()
    peers = []
    for dy in range(NY):
        for dc in range(2):
            if dy or dc:
                peers.append((fid(x, z, lax.rem(c + dc, 2)), m4(y + dy)))
    for dx in range(1, NX):
        for dc in range(2):
            peers.append((fid(m4(x + dx), z, lax.rem(c + dc, 2)), y))
    for dz in range(1, NZ):
        peers.append((fid(x, m8(z + dz), c), y))
    for ff, yy in peers:
        pl.semaphore_signal(barrier, inc=1, device_id={"fsdp": ff, "dp": yy}, device_id_type=MESH)
    pl.semaphore_wait(barrier, len(peers))

    for dy in (2, 1, 3, 0):
        for kind in range(2):
            yy = m4(y + dy)
            send(
                send_ref.at[kind, yy], st1.at[y * 2 + c], s1s.at[kind * 4 + dy], s1r.at[y * 2 + c],
                fid(x, z, kind), yy, own=(c == kind) if dy == 0 else None,
            )

    def dequant_cols(codes, slot, s0):
        def body(i, carry):
            rows = pl.ds(pl.multiple_of(i * 128, 128), 128)
            wgu[slot, rows, 0:128] = (codes[rows, 0:128].astype(F32) * sc_ref[i, s0]).astype(BF)
            wgu[slot, rows, 128:256] = (codes[rows, 128:256].astype(F32) * sc_ref[i, s0 + 1]).astype(BF)
            return carry

        lax.fori_loop(0, 14, body, 0)

    sib = fid(x, z, o)
    loads[0].wait()
    dequant_cols(gcv, c, 0)
    wgu[c, KP : KP + R, :] = gl_ref[...]
    wgu[c, KP + R :, :] = jnp.zeros((R, H), BF)
    send(wgu.at[c], wgu.at[c], wss.at[0], wsr.at[0], sib, y)
    loads[1].wait()
    dequant_cols(ucv, 2 + c, 2)
    wgu[2 + c, KP : KP + R, :] = jnp.zeros((R, H), BF)
    wgu[2 + c, KP + R :, :] = ul_ref[...]
    send(wgu.at[2 + c], wgu.at[2 + c], wss.at[1], wsr.at[1], sib, y)
    loads[2].wait()

    def dequant_down(i, carry):
        cols = pl.ds(pl.multiple_of(i * 128, 128), 128)
        wd[c, 0:128, cols] = (dcv[0:128, cols].astype(F32) * sc_ref[i, 4]).astype(BF)
        wd[c, 128:256, cols] = (dcv[128:256, cols].astype(F32) * sc_ref[i, 5]).astype(BF)
        return carry

    lax.fori_loop(0, 14, dequant_down, 0)
    wd[c, :, KP:KE] = jnp.zeros((H, EX), BF)
    wd[c, :, KP : KP + R] = de_ref[...]
    send(wd.at[c], wd.at[c], wss.at[2], wsr.at[2], sib, y)

    for i in range(8):
        wait(st1.at[i], s1r.at[i])
    got = st1[...].reshape(128, H)
    row8 = lax.broadcasted_iota(jnp.int32, (G, 128), 0) * 8
    col = lax.broadcasted_iota(jnp.int32, (G, 128), 1)
    for j in range(8):
        pick = (col == row8 + j).astype(F32).astype(BF)
        v = mm(pick, got).astype(BF)
        if j < 7:
            aa[z, x, :, j * 256 : (j + 1) * 256] = v
        else:
            aa[z, x, :, KP:KE] = v[:, :EX]

    flag = jnp.where(y == 0, 1.0, 0.0).astype(F32)

    def masked(v):
        return (v.astype(F32) * flag).astype(BF)

    def have(zz, xx):
        wait(aa.at[zz, xx], agr.at[zz * 4 + xx])

    def fwd(zz, xx, tz, tx, ssem):
        send(aa.at[zz, xx], aa.at[zz, xx], ssem, agr.at[zz * 4 + xx], fid(tx, tz, c), y)

    zr, zl = m8(z + 1), m8(z + 7)
    xrt, xlt = m4(x + 1), m4(x + 3)
    xf, zf = m4(x + 2), m8(z + 4)

    def weights():
        wait(wgu.at[o], wsr.at[0])
        wait(wgu.at[2 + o], wsr.at[1])
        wait(wd.at[o], wsr.at[2])

    def front0(zs):
        def body(b, carry):
            a = jnp.concatenate([aa[zz].reshape(64, KE) for zz in zs], axis=0)
            acc = mm(a[:, :KP], wgu[b, 0:KP, :]) + mm(masked(a[:, KP:]), wgu[b, KP:KE, :])
            acc = acc.astype(BF)
            for i, zz in enumerate(zs):
                part[zz, :, b] = acc[i * 64 : (i + 1) * 64].reshape(4, G, H)
            return carry

        lax.fori_loop(0, 4, body, 0)
        for zz in zs:
            cc, q = lax.div(zz, 4), m4(zz)
            for xx in range(NX):
                yy = m4(zz + xx)
                send(
                    part.at[zz, xx], rgu.at[y, q], gus.at[zz * 4 + xx], gur.at[y * 4 + q],
                    fid(x, z, cc), yy, own=jnp.logical_and(yy == y, cc == 0),
                )

    def front1(xx):
        def body(b, carry):
            a = aa[:, xx].reshape(128, KE)
            acc = mm_nt(a[:, :KP], wd[b, :, 0:KP]) + mm_nt(masked(a[:, KP:]), wd[b, :, KP:KE])
            parth[xx, :, b] = acc.astype(BF).reshape(8, G, H)
            return carry

        lax.fori_loop(0, 2, body, 0)
        for zz in range(NZ):
            cc, q, yy = zz // 4, zz % 4, m4(xx + zz)
            send(
                parth.at[xx, zz], rh.at[y, q], hs.at[xx * 8 + zz], hr.at[y * 4 + q],
                fid(x, z, cc), yy, own=(yy == y) if cc == 1 else None,
            )

    @pl.when(c == 0)
    def _():
        keep = len(pending)
        before = pending[:]
        pending.clear()
        fwd(z, x, z, xrt, ags.at[2, z * 4 + x])
        fwd(z, x, z, xlt, ags.at[3, z * 4 + x])
        fwd(z, x, z, xf, agx)
        fwd(z, x, zr, x, ags.at[0, z * 4 + x])
        fwd(z, x, zl, x, ags.at[1, z * 4 + x])
        for xx in (xrt, xlt, xf):
            have(z, xx)
            fwd(z, xx, zr, x, ags.at[0, z * 4 + xx])
            fwd(z, xx, zl, x, ags.at[1, z * 4 + xx])
        weights()
        front0([z])
        for k in range(1, 4):
            za, zb = m8(z + 8 - k), m8(z + k)
            for i, xx in enumerate((x, xrt, xlt, xf)):
                have(za, xx)
                if k < 3 or i < 2:
                    fwd(za, xx, zr, x, ags.at[0, za * 4 + xx])
                have(zb, xx)
                if k < 3 or i >= 2:
                    fwd(zb, xx, zl, x, ags.at[1, zb * 4 + xx])
            front0([za, zb])
        for xx in range(NX):
            have(zf, xx)
        front0([zf])
        drain()
        pending.extend(before)

    @pl.when(c == 1)
    def _():
        before = pending[:]
        pending.clear()
        fwd(z, x, zr, x, ags.at[0, z * 4 + x])
        fwd(z, x, zl, x, ags.at[1, z * 4 + x])

        def spread(zz):
            fwd(zz, x, z, xrt, ags.at[2, zz * 4 + x])
            fwd(zz, x, z, xlt, ags.at[3, zz * 4 + x])

        def xstep(i):
            zz = m8(z + ORDER[i])
            have(zz, xlt)
            if i % 2 == 0:
                fwd(zz, xlt, z, xrt, ags.at[2, zz * 4 + xlt])
            have(zz, xrt)
            if i % 2 == 1:
                fwd(zz, xrt, z, xlt, ags.at[3, zz * 4 + xrt])

        spread(z)
        for k in range(1, 4):
            za, zb = m8(z + 8 - k), m8(z + k)
            have(za, x)
            fwd(za, x, zr, x, ags.at[0, za * 4 + x])
            spread(za)
            have(zb, x)
            if k < 3:
                fwd(zb, x, zl, x, ags.at[1, zb * 4 + x])
            spread(zb)
            for i in {1: (0,), 2: (1, 2), 3: (3, 4)}[k]:
                xstep(i)
        have(zf, x)
        spread(zf)
        weights()
        front1(x)
        for i in (5, 6, 7):
            xstep(i)
        front1(xlt)
        front1(xrt)
        for zz in range(NZ):
            have(zz, xf)
        front1(xf)
        drain()
        pending.extend(before)

    send(aa.at[:, :, :, pl.ds(KP, EX)], ext, exs, exr, sib, y)

    def middle(q, carry):
        for s in range(NY):
            wait(rgu.at[s, q], gur.at[s * 4 + q])
            wait(rh.at[s, q], hr.at[s * 4 + q])
        for b in range(2):
            g = rgu[0, q, b].astype(F32)
            u = rgu[0, q, 2 + b].astype(F32)
            h = rh[0, q, b].astype(F32)
            for s in range(1, NY):
                g += rgu[s, q, b].astype(F32)
                u += rgu[s, q, 2 + b].astype(F32)
                h += rh[s, q, b].astype(F32)
            sig = jax.nn.sigmoid(g)
            act = g * sig
            hb[q, b] = (act * u).astype(BF)
            gb[q, b] = (h * u * sig * (1.0 + g * (1.0 - sig))).astype(BF)
            gb[q, 2 + b] = (h * act).astype(BF)
        return carry

    lax.fori_loop(0, 4, middle, 0)
    for dy in (2, 1, 3, 0):
        yy = m4(y + dy)
        send(gb, gall.at[c * 4 + y], gbs.at[dy], gallr.at[c * 4 + y], fid(x, z, 1), yy,
             own=(c == 1) if dy == 0 else None)
        send(hb, hall.at[c * 4 + y], hbs.at[dy], hallr.at[c * 4 + y], fid(x, z, 0), yy,
             own=(c == 0) if dy == 0 else None)

    wait(ext, exr)
    for i in range(8):
        for q in range(4):
            zz = (i // 4) * 4 + q
            extp[(i * 4 + q) * G : (i * 4 + q + 1) * G, :] = ext[zz, (i % 4 + 8 - zz) % 4]

    def ring(d, slot, v, tgt):
        rss[d, slot] = v.astype(BF)
        send(rss.at[d, slot], rsr.at[d, slot], rsss.at[d, slot], rsrs.at[d, slot], tgt, y)

    def come(d, slot):
        wait(rsr.at[d, slot], rsrs.at[d, slot])
        return rsr[d, slot].astype(F32)

    def total(n):
        v = xr[0].astype(F32)
        for i in range(1, n):
            v += xr[i].astype(F32)
        return v

    def pack(fin):
        m = lax.broadcasted_iota(jnp.int32, (128, G), 0)
        r8 = lax.broadcasted_iota(jnp.int32, (128, G), 1) * 8
        acc = jnp.zeros((128, H), F32)
        for j in range(7):
            put = (m == r8 + j).astype(F32).astype(BF)
            acc += mm(put, fin[:, j * 256 : (j + 1) * 256])
        msg[...] = acc.astype(BF).reshape(8, G, H)

    @pl.when(c == 0)
    def _():
        before = pending[:]
        pending.clear()
        for i in range(8):
            wait(hall.at[i], hallr.at[i])

        def out0(ts):
            def rows(kb):
                return jnp.concatenate(
                    [hall[lax.div(t, 4) * 4 + m4(t + xx), m4(t), kb] for t in ts for xx in range(NX)], axis=0
                )

            def body(nb, carry):
                cols = pl.ds(pl.multiple_of(nb * NB, 128), NB)
                po[0 : 64 * len(ts), cols] = mm(rows(0), wd[0, :, cols]) + mm(rows(1), wd[1, :, cols])
                return carry

            lax.fori_loop(0, KE // NB, body, 0)

        right, left = fid(x, zr, 0), fid(x, zl, 0)
        out0([zf])
        for xx in range(2):
            ring(0, xx, po[xx * G : (xx + 1) * G, :], right)
            ring(1, xx + 2, po[(xx + 2) * G : (xx + 3) * G, :], left)
        for b in range(2):
            grad = mm_tn(hall[:, :, b].reshape(512, H), extp[...])
            dep[b] = grad
        send(dep.at[1], der, las.at[0], lar.at[0], sib, y)
        dde_out[...] = dep[0][:, :R]
        for s in range(1, 4):
            out0([m8(z + 4 - s), m8(z + 4 + s)])
            for xx in range(NX):
                v = po[xx * G : (xx + 1) * G, :]
                if s > 1 or xx < 2:
                    v = v + come(0, (s - 1) * 4 + xx)
                ring(0, s * 4 + xx, v, right)
                v = po[(4 + xx) * G : (5 + xx) * G, :]
                if s > 1 or xx >= 2:
                    v = v + come(1, (s - 1) * 4 + xx)
                ring(1, s * 4 + xx, v, left)
        out0([z])
        for xx in range(NX):
            v = po[xx * G : (xx + 1) * G, :] + come(0, 12 + xx) + come(1, 12 + xx)
            xs[xx] = v.astype(BF)
            send(xs.at[xx], xr.at[x], xss.at[xx], xrs.at[x], fid(xx, z, 0), y, own=(x == xx))
        loads[5].wait()
        for i in range(NX):
            wait(xr.at[i], xrs.at[i])
        fin = total(NX)
        mid = fin[:, KP:KE].astype(BF)
        smx[...] = mid
        pack((fin[:, :KP] + mm(mid[:, :R], dlv[...])).astype(BF))
        loads[3].wait()
        loads[4].wait()
        drain()
        pending.extend(before)

    @pl.when(c == 1)
    def _():
        before = pending[:]
        pending.clear()
        for i in range(8):
            wait(gall.at[i], gallr.at[i])

        def out1(t):
            def rows(b):
                return jnp.concatenate(
                    [gall[(zz // 4) * 4 + m4(t + zz), zz % 4, b] for zz in range(NZ)], axis=0
                )

            def body(nb, carry):
                cols = pl.ds(pl.multiple_of(nb * NB, 128), NB)
                acc = mm_nt(rows(0), wgu[0, cols, :])
                for b in range(1, 4):
                    acc += mm_nt(rows(b), wgu[b, cols, :])
                po[:, cols] = acc
                return carry

            lax.fori_loop(0, KE // NB, body, 0)

        right, left = fid(xrt, z, 1), fid(xlt, z, 1)
        out1(xf)
        for zz in range(4):
            ring(0, zz, po[zz * G : (zz + 1) * G, :], right)
            ring(1, zz + 4, po[(zz + 4) * G : (zz + 5) * G, :], left)
        out1(xrt)
        for zz in range(NZ):
            v = po[zz * G : (zz + 1) * G, :]
            if zz < 4:
                v = v + come(0, zz)
            ring(0, 8 + zz, v, right)
        out1(xlt)
        for zz in range(NZ):
            v = po[zz * G : (zz + 1) * G, :]
            if zz >= 4:
                v = v + come(1, zz)
            ring(1, 8 + zz, v, left)
        for b in range(4):
            grad = mm_tn(extp[...], gall[:, :, b].reshape(512, H))
            dlp[b] = grad[0:R] if b < 2 else grad[R:EX]
        send(dlp.at[0], dlr.at[0], las.at[0], lar.at[0], sib, y)
        send(dlp.at[2], dlr.at[1], las.at[1], lar.at[1], sib, y)
        dgl_out[...] = dlp[1]
        dul_out[...] = dlp[3]
        out1(x)
        for zz in range(NZ):
            v = po[zz * G : (zz + 1) * G, :] + come(0, 8 + zz) + come(1, 8 + zz)
            xs[zz] = v.astype(BF)
            send(xs.at[zz], xr.at[z], xss.at[zz], xrs.at[z], fid(x, zz, 1), y, own=(z == zz))
        loads[3].wait()
        loads[4].wait()
        for i in range(NZ):
            wait(xr.at[i], xrs.at[i])
        fin = total(NZ)
        mid = fin[:, KP:KE].astype(BF)
        smx[...] = mid
        back = mm_nt(mid[:, :R], gev[...]) + mm_nt(mid[:, R:], uev[...])
        pack((fin[:, :KP] + back).astype(BF))
        loads[5].wait()
        drain()
        pending.extend(before)

    send(smx, sm1.at[x], t0s, t0r.at[x], fid(y, z, o), y)
    for dy in (2, 1, 3, 0):
        for cc in range(2):
            yy = m4(y + dy)
            send(
                msg.at[yy * 2 + cc], rowsr.at[c, y], msgs.at[dy * 2 + cc], rowss.at[c, y],
                fid(x, z, cc), yy, own=(c == cc) if dy == 0 else None,
            )

    @pl.when(x == y)
    def _():
        before = pending[:]
        pending.clear()
        for i in range(NX):
            wait(sm1.at[i], t0r.at[i])
        for dz in (4, 3, 5, 2, 6, 1, 7):
            send(sm1, sm2.at[z], t1s.at[dz], t1r.at[z], fid(x, m8(z + dz), c), y)
        sm2[z] = sm1[...]
        for dz in range(1, NZ):
            zz = m8(z + dz)
            wait(sm2.at[zz], t1r.at[zz])
        small = sm2[...].reshape(512, EX)

        def body(nb, carry):
            cols = pl.ds(pl.multiple_of(nb * 256, 128), 256)
            res[pl.ds(pl.multiple_of(nb * 256, 128), 256), :] = mm_tn(
                aa[:, :, :, cols].reshape(512, 256), small
            )
            return carry

        lax.fori_loop(0, 7, body, 0)
        for cc in range(2):
            mb[cc] = res[pl.ds(pl.multiple_of(z * 224 + cc * 112, 8), 112), :].astype(BF)
        for dy in (2, 1, 3, 0):
            for cc in range(2):
                send(
                    mb.at[cc], fd.at[c], t3s.at[dy * 2 + cc], t3r.at[c], fid(x, z, cc), m4(y + dy),
                    own=(c == cc) if dy == 0 else None,
                )
        drain()
        pending.extend(before)

    @pl.when(c == 0)
    def _():
        wait(dlr.at[0], lar.at[0])
        wait(dlr.at[1], lar.at[1])
        dgl_out[...] = dlr[0]
        dul_out[...] = dlr[1]

    @pl.when(c == 1)
    def _():
        wait(der, lar.at[0])
        dde_out[...] = der[:, :R]

    for k in range(2):
        for s in range(NY):
            wait(rowsr.at[k, s], rowss.at[k, s])
    rows_out[...] = rowsr[...]
    wait(fd.at[0], t3r.at[0])
    wait(fd.at[1], t3r.at[1])
    v = fd[0].astype(F32)
    dge_out[...] = v[:, :R]
    due_out[...] = v[:, R:]
    ddl_out[...] = fd[1].astype(F32)
    drain()


def dma(*shape):
    return pltpu.SemaphoreType.DMA(shape)


def on_device(
    tokens, grad_out, gate_codes, gate_scales, up_codes, up_scales, down_codes, down_scales,
    gate_enter, gate_leave, up_enter, up_leave, down_enter, down_leave,
):
    gate_own = mm(tokens, gate_enter).astype(BF)
    up_own = mm(tokens, up_enter).astype(BF)
    back_own = mm_nt(grad_out, down_leave).astype(BF)
    ext = jnp.stack(
        [jnp.concatenate([gate_own, up_own], 1), jnp.concatenate([back_own, jnp.zeros_like(back_own)], 1)]
    )
    body = jnp.stack([tokens, grad_out]).reshape(2, 2, NY, KP)
    ext = jnp.broadcast_to(ext[:, :, None, :], (2, 2, NY, EX))
    pad = jnp.zeros((2, 2, NY, 2048 - KE), BF)
    sends = jnp.concatenate([body, ext, pad], axis=-1).transpose(0, 2, 1, 3).reshape(2, NY, G, H)
    scales = jnp.concatenate([gate_scales, up_scales, down_scales.T], axis=1).astype(F32)

    vm = pl.BlockSpec(memory_space=pltpu.VMEM)
    sm = pl.BlockSpec(memory_space=pltpu.SMEM)
    hb = pl.BlockSpec(memory_space=pl.ANY)
    V = pltpu.VMEM
    scratch = [
        V((KP, H), BF), V((KP, H), BF), V((H, KP), BF), V((KP, R), BF), V((KP, R), BF), V((R, KP), BF), dma(6),
        V((8, G, H), BF), dma(8), dma(8),
        V((4, KE, H), BF), V((2, H, KE), BF), dma(3), dma(3),
        V((NZ, NX, G, KE), BF), dma(4, 32), pltpu.SemaphoreType.DMA, dma(32),
        V((NZ, NX, G, EX), BF), V((512, EX), BF), pltpu.SemaphoreType.DMA, pltpu.SemaphoreType.DMA,
        V((NZ, NX, 4, G, H), BF), dma(32), V((NY, 4, 4, G, H), BF), dma(16),
        V((NX, NZ, 2, G, H), BF), dma(32), V((NY, 4, 2, G, H), BF), dma(16),
        V((4, 2, G, H), BF), dma(4), V((8, 4, 2, G, H), BF), dma(8),
        V((4, 4, G, H), BF), dma(4), V((8, 4, 4, G, H), BF), dma(8),
        V((128, KE), F32), V((2, 16, G, KE), BF), dma(2, 16), V((2, 16, G, KE), BF), dma(2, 16),
        V((8, G, KE), BF), dma(8), V((8, G, KE), BF), dma(8),
        V((8, G, H), BF), dma(8), V((2, NY, G, H), BF), dma(2, NY),
        V((G, EX), BF), V((NX, G, EX), BF), V((NZ, NX, G, EX), BF),
        pltpu.SemaphoreType.DMA, dma(NX), dma(NZ), dma(NZ),
        V((KP, EX), F32), V((2, 112, EX), BF), V((2, 112, EX), BF), dma(8), dma(2),
        V((4, R, H), F32), V((2, R, H), F32), V((2, H, EX), F32), V((H, EX), F32), dma(2), dma(2),
    ]
    S = jax.ShapeDtypeStruct
    rows, dge, due, ddl, dgl, dul, dde = pl.pallas_call(
        kernel,
        out_shape=[
            S((2, NY, G, H), BF), S((112, R), F32), S((112, R), F32), S((112, EX), F32),
            S((R, H), F32), S((R, H), F32), S((H, R), F32),
        ],
        in_specs=[vm, sm, hb, hb, hb, vm, vm, vm, hb, hb, hb],
        out_specs=[vm] * 7,
        scratch_shapes=scratch,
        compiler_params=pltpu.CompilerParams(
            collective_id=0, has_side_effects=True, vmem_limit_bytes=48 * 1024 * 1024
        ),
        name="lora_ffn_step",
    )(
        sends, scales, gate_codes, up_codes, down_codes, gate_leave, up_leave, down_enter,
        gate_enter, up_enter, down_leave,
    )
    rows = rows.reshape(2, NY, 2, 2048)[..., :KP].transpose(0, 2, 1, 3).reshape(2, 2, NY * KP)
    return rows[0], rows[1], dge, dgl, due, dul, dde, ddl[:, :R].T


def solution(mesh):
    return jax.shard_map(
        on_device,
        mesh=mesh,
        in_specs=(
            P(("fsdp", "dp"), None),
            P(("fsdp", "dp"), None),
            P("dp", "fsdp"),
            P("dp", "fsdp"),
            P("dp", "fsdp"),
            P("dp", "fsdp"),
            P("fsdp", "dp"),
            P("fsdp", "dp"),
            P(),
            P(None, "fsdp"),
            P(),
            P(None, "fsdp"),
            P("fsdp", None),
            P(),
        ),
        out_specs=(
            P(("fsdp", "dp"), None),
            P(("fsdp", "dp"), None),
            P("fsdp", None),
            P(None, "fsdp"),
            P("fsdp", None),
            P(None, "fsdp"),
            P("fsdp", None),
            P(None, "fsdp"),
        ),
        check_vma=False,
    )
```

```python
import jax
import jax.numpy as jnp
from jax import lax
from jax.experimental import pallas as pl
from jax.experimental.pallas import tpu as pltpu
from jax.sharding import PartitionSpec as P

NX, NZ, NY = 4, 8, 4
KP, KE, EX = 1792, 1920, 128
G, H, R = 16, 256, 64
NB = 384
BF, F32 = jnp.bfloat16, jnp.float32
MESH = pl.DeviceIdType.MESH
ORDER = (0, 7, 1, 6, 2, 5, 3, 4)


def mm(a, b):
    return jnp.dot(a, b, preferred_element_type=F32)


def mm_nt(a, b):
    return lax.dot_general(a, b, (((1,), (1,)), ((), ())), preferred_element_type=F32)


def mm_tn(a, b):
    return lax.dot_general(a, b, (((0,), (0,)), ((), ())), preferred_element_type=F32)


def kernel(
    tok_ref, gout_ref, sc_ref, gc_hbm, uc_hbm, dc_hbm, gl_ref, ul_ref, det_ref, get_hbm, uet_hbm, dl_hbm,
    rows_out, fd_out, dla_out,
    gcv, ucv, dcv, gev, dlv, ldsem,
    sf, sends, st1, s1r,
    wgu, wd, wsr,
    aa, agr,
    ext, extp, exr,
    part, rgu, gur,
    parth, rh, hr,
    hb, hall, hallr,
    gb, gall, gallr,
    po, pq, rss, rsr, rsrs,
    xs, xr, xrs,
    msg, rowsr, rowss,
    sp, sa, sar, sb, sc8, sc8r, sd, se, ser, smm, smr,
    res, mb, fd, t3r,
    dlp, dlr, lar,
    pool_all, pool_core, pool_xy,
):
    f = lax.axis_index("fsdp")
    y = lax.axis_index("dp")
    x = lax.div(f, 16)
    z = lax.rem(lax.div(f, 2), 8)
    c = lax.rem(f, 2)
    o = 1 - c

    def fid(xx, zz, cc):
        return xx * 16 + zz * 2 + cc

    def m4(v):
        return lax.rem(v, 4)

    def m8(v):
        return lax.rem(v, 8)

    zp = [m8(z + k) for k in range(NZ)]
    xp = [m4(x + k) for k in range(NX)]
    yp = [m4(y + k) for k in range(NY)]

    def rcopy(src, dst, ssem, rsem, ff, yy):
        return pltpu.make_async_remote_copy(
            src_ref=src, dst_ref=dst, send_sem=ssem, recv_sem=rsem,
            device_id={"fsdp": ff, "dp": yy}, device_id_type=MESH,
        )

    def wait(ref, sem):
        pltpu.make_async_copy(ref, ref, sem).wait()

    scopes = {
        "all": (pool_all, [], None),
        0: (pool_core, [], lambda: c == 0),
        1: (pool_core, [], lambda: c == 1),
        "xy0": (pool_xy, [], lambda: jnp.logical_and(c == 0, x == y)),
        "xy1": (pool_xy, [], lambda: jnp.logical_and(c == 1, x == y)),
    }
    scope = ["all"]

    def within(name, cond, fn):
        scope.append(name)
        pl.when(cond)(fn)
        scope.pop()

    def send(src, dst, rsem, ff, yy, own=None):
        pool, pending, _ = scopes[scope[-1]]
        ssem = pool.at[len(pending)]
        pending.append((src.shape, own))
        if own is None:
            rcopy(src, dst, ssem, rsem, ff, yy).start()
            return

        @pl.when(own())
        def _():
            pltpu.make_async_copy(src, dst, rsem).start()

        @pl.when(jnp.logical_not(own()))
        def _():
            rcopy(src, dst, ssem, rsem, ff, yy).start()

    def drain(name, now=False):
        pool, pending, cond = scopes[name]

        def body():
            like = {
                (G, H): sp.at[0], (KE, H): wgu.at[0], (H, KE): wd.at[0], (G, KE): aa.at[0, 0],
                (NZ, NX, G, EX): ext, (4, G, H): part.at[0, 0], (2, G, H): parth.at[0, 0],
                (4, G, EX): smm.at[0], (EX, EX): mb.at[0], (R, H): dlp.at[0],
            }
            for i, (shape, own) in enumerate(pending):
                if own is None:
                    wait(like[shape], pool.at[i])
                else:
                    @pl.when(jnp.logical_not(own()))
                    def _(shape=shape, i=i):
                        wait(like[shape], pool.at[i])

        if cond is None or now:
            body()
            pending.clear()
        else:
            pl.when(cond())(body)

    loads = [
        pltpu.make_async_copy(get_hbm, gev.at[pl.ds(0, R)], ldsem.at[0]),
        pltpu.make_async_copy(uet_hbm, gev.at[pl.ds(R, R)], ldsem.at[1]),
        pltpu.make_async_copy(dl_hbm, dlv.at[pl.ds(0, R)], ldsem.at[2]),
        pltpu.make_async_copy(gc_hbm, gcv, ldsem.at[3]),
        pltpu.make_async_copy(uc_hbm, ucv, ldsem.at[4]),
        pltpu.make_async_copy(dc_hbm, dcv, ldsem.at[5]),
    ]
    for ld in loads:
        ld.start()

    barrier = pltpu.get_barrier_semaphore()
    peers = []
    for dy in range(NY):
        for dc in range(2):
            if dy or dc:
                peers.append((fid(x, z, lax.rem(c + dc, 2)), yp[dy]))
    for dx in range(1, NX):
        peers.append((fid(xp[dx], z, c), y))
    for dz in range(1, NZ):
        peers.append((fid(x, zp[dz], c), y))
    for ff, yy in peers:
        pl.semaphore_signal(barrier, inc=1, device_id={"fsdp": ff, "dp": yy}, device_id_type=MESH)

    dlv[R:EX, :] = jnp.zeros((R, NY * KP), BF)
    for kind, ref in enumerate((tok_ref, gout_ref)):
        v = ref[...].astype(F32)
        v16 = jnp.concatenate([v, jnp.zeros((14, NY * KP), F32)], axis=0).astype(BF)
        for yy in range(NY):
            for t in range(2):
                for j in range(7):
                    sf[kind, yy, t * 8 + j : t * 8 + j + 1, :] = v[
                        t : t + 1, yy * KP + j * 256 : yy * KP + (j + 1) * 256
                    ]
        if kind == 0:
            loads[0].wait()
            loads[1].wait()
            e = mm_nt(v16, gev[...])
        else:
            loads[2].wait()
            e = mm_nt(v16, dlv[...])
        for yy in range(NY):
            for t in range(2):
                sf[kind, yy, t * 8 + 7 : t * 8 + 8, :] = jnp.concatenate(
                    [e[t : t + 1], jnp.zeros((1, EX), F32)], axis=1
                )
    sends[...] = sf[...].astype(BF)
    pl.semaphore_wait(barrier, len(peers))

    for dy in (2, 1, 3, 0):
        for kind in range(2):
            send(
                sends.at[kind, yp[dy]], st1.at[y * 2 + c], s1r.at[y * 2 + c],
                fid(x, z, kind), yp[dy], own=(lambda kind=kind: c == kind) if dy == 0 else None,
            )

    def dequant_cols(codes, slot, s0):
        def body(i, carry):
            rows = pl.ds(pl.multiple_of(i * 128, 128), 128)
            wgu[slot, rows, 0:128] = (codes[rows, 0:128].astype(F32) * sc_ref[s0, i]).astype(BF)
            wgu[slot, rows, 128:256] = (codes[rows, 128:256].astype(F32) * sc_ref[s0 + 1, i]).astype(BF)
            return carry

        lax.fori_loop(0, 14, body, 0)

    sib = fid(x, z, o)
    loads[3].wait()
    dequant_cols(gcv, c, 0)
    wgu[c, KP : KP + R, :] = gl_ref[...]
    wgu[c, KP + R :, :] = jnp.zeros((R, H), BF)
    send(wgu.at[c], wgu.at[c], wsr.at[0], sib, y)
    loads[4].wait()
    dequant_cols(ucv, 2 + c, 2)
    wgu[2 + c, KP : KP + R, :] = jnp.zeros((R, H), BF)
    wgu[2 + c, KP + R :, :] = ul_ref[...]
    send(wgu.at[2 + c], wgu.at[2 + c], wsr.at[1], sib, y)
    loads[5].wait()

    def dequant_down(i, carry):
        cols = pl.ds(pl.multiple_of(i * 128, 128), 128)
        wd[c, 0:128, cols] = (dcv[0:128, cols].astype(F32) * sc_ref[4, i]).astype(BF)
        wd[c, 128:256, cols] = (dcv[128:256, cols].astype(F32) * sc_ref[5, i]).astype(BF)
        return carry

    lax.fori_loop(0, 14, dequant_down, 0)
    det = jnp.concatenate([det_ref[...].astype(F32), jnp.zeros((R, H), F32)], axis=0)
    wd[c, :, KP:KE] = det.T.astype(BF)
    send(wd.at[c], wd.at[c], wsr.at[2], sib, y)

    for i in range(8):
        wait(st1.at[i], s1r.at[i])
    got = st1[...].reshape(128, H)
    row8 = lax.broadcasted_iota(jnp.int32, (G, 128), 0) * 8
    col = lax.broadcasted_iota(jnp.int32, (G, 128), 1)
    for j in range(8):
        pick = (col == row8 + j).astype(F32).astype(BF)
        v = mm(pick, got).astype(BF)
        if j < 7:
            aa[z, x, :, j * 256 : (j + 1) * 256] = v
        else:
            aa[z, x, :, KP:KE] = v[:, :EX]

    flag = jnp.where(y == 0, 1.0, 0.0).astype(F32)

    def masked(v):
        return (v.astype(F32) * flag).astype(BF)

    def have(zz, xx):
        wait(aa.at[zz, xx], agr.at[zz * 4 + xx])

    def fwd(zz, xx, tz, tx):
        send(aa.at[zz, xx], aa.at[zz, xx], agr.at[zz * 4 + xx], fid(tx, tz, c), y)

    zr, zl, zf = zp[1], zp[7], zp[4]
    xrt, xlt, xf = xp[1], xp[3], xp[2]

    def weights():
        wait(wgu.at[o], wsr.at[0])
        wait(wgu.at[2 + o], wsr.at[1])
        wait(wd.at[o], wsr.at[2])

    def front0(zs):
        def body(b, carry):
            a = jnp.concatenate([aa[zz].reshape(64, KE) for zz in zs], axis=0)
            acc = mm(a[:, :KP], wgu[b, 0:KP, :]) + mm(masked(a[:, KP:]), wgu[b, KP:KE, :])
            acc = acc.astype(BF)
            for i, zz in enumerate(zs):
                part[zz, :, b] = acc[i * 64 : (i + 1) * 64].reshape(4, G, H)
            return carry

        lax.fori_loop(0, 4, body, 0)
        for zz in zs:
            for xx in range(NX):
                send(
                    part.at[zz, xx], rgu.at[y, m4(zz)], gur.at[y * 4 + m4(zz)],
                    fid(x, z, lax.div(zz, 4)), m4(zz + xx),
                    own=lambda zz=zz, xx=xx: jnp.logical_and(m4(zz + xx) == y, zz < 4),
                )

    def front1(xx):
        def body(b, carry):
            a = aa[:, xx].reshape(128, KE)
            acc = mm_nt(a[:, :KP], wd[b, :, 0:KP]) + mm_nt(masked(a[:, KP:]), wd[b, :, KP:KE])
            parth[xx, :, b] = acc.astype(BF).reshape(8, G, H)
            return carry

        lax.fori_loop(0, 2, body, 0)
        for zz in range(NZ):
            send(
                parth.at[xx, zz], rh.at[y, zz % 4], hr.at[y * 4 + zz % 4],
                fid(x, z, zz // 4), m4(xx + zz),
                own=(lambda xx=xx, zz=zz: m4(xx + zz) == y) if zz >= 4 else None,
            )

    def gather0():
        fwd(z, x, zr, x)
        fwd(z, x, zl, x)
        fwd(z, x, z, xf)
        fwd(z, x, z, xrt)
        fwd(z, x, z, xlt)
        for xx in (xrt, xlt, xf):
            have(z, xx)
            fwd(z, xx, zr, x)
            fwd(z, xx, zl, x)
        weights()
        front0([z])
        for k in range(1, 4):
            za, zb = zp[8 - k], zp[k]
            for i, xx in enumerate((x, xrt, xlt, xf)):
                have(za, xx)
                if k < 3 or i < 2:
                    fwd(za, xx, zr, x)
                have(zb, xx)
                if k < 3 or i >= 2:
                    fwd(zb, xx, zl, x)
            front0([za, zb])
        for xx in range(NX):
            have(zf, xx)
        send(aa.at[:, :, :, pl.ds(KP, EX)], ext, exr, sib, y)
        front0([zf])

    def gather1():
        fwd(z, x, zr, x)
        fwd(z, x, zl, x)

        def spread(zz):
            fwd(zz, x, z, xrt)
            fwd(zz, x, z, xlt)

        def xstep(i):
            zz = zp[ORDER[i]]
            have(zz, xlt)
            if i % 2 == 0:
                fwd(zz, xlt, z, xrt)
            have(zz, xrt)
            if i % 2 == 1:
                fwd(zz, xrt, z, xlt)

        spread(z)
        for k in range(1, 4):
            za, zb = zp[8 - k], zp[k]
            have(za, x)
            fwd(za, x, zr, x)
            spread(za)
            have(zb, x)
            if k < 3:
                fwd(zb, x, zl, x)
            spread(zb)
            for i in {1: (0,), 2: (1, 2), 3: (3, 4)}[k]:
                xstep(i)
        have(zf, x)
        spread(zf)
        weights()
        front1(x)
        for i in (5, 6, 7):
            xstep(i)
        front1(xlt)
        front1(xrt)
        for zz in range(NZ):
            have(zz, xf)
        send(aa.at[:, :, :, pl.ds(KP, EX)], ext, exr, sib, y)
        front1(xf)

    within(0, c == 0, gather0)
    within(1, c == 1, gather1)

    def middle(q, carry):
        for s in range(NY):
            wait(rgu.at[s, q], gur.at[s * 4 + q])
            wait(rh.at[s, q], hr.at[s * 4 + q])
        for b in range(2):
            g = rgu[0, q, b].astype(F32)
            u = rgu[0, q, 2 + b].astype(F32)
            h = rh[0, q, b].astype(F32)
            for s in range(1, NY):
                g += rgu[s, q, b].astype(F32)
                u += rgu[s, q, 2 + b].astype(F32)
                h += rh[s, q, b].astype(F32)
            sig = jax.nn.sigmoid(g)
            act = g * sig
            hb[q, b] = (act * u).astype(BF)
            gb[q, b] = (h * u * sig * (1.0 + g * (1.0 - sig))).astype(BF)
            gb[q, 2 + b] = (h * act).astype(BF)
        return carry

    lax.fori_loop(0, 4, middle, 0)
    blk = c * 4 + y
    for i in range(4):
        qh = m4(z + (0, 3, 1, 2)[i])
        qg = m4(y + 8 - x - (2, 1, 3, 0)[i])
        for dy in (2, 1, 3, 0):
            send(gb.at[qg], gall.at[blk, qg], gallr.at[blk * 4 + qg], fid(x, z, 1), yp[dy],
                 own=(lambda: c == 1) if dy == 0 else None)
            send(hb.at[qh], hall.at[blk, qh], hallr.at[blk * 4 + qh], fid(x, z, 0), yp[dy],
                 own=(lambda: c == 0) if dy == 0 else None)

    def small_a():
        mids = jnp.zeros((64, EX), F32)
        backs = jnp.zeros((64, EX), F32)
        for b in range(2):
            mids += mm(hb[:, b].reshape(64, H), wd[b, :, KP:KE])
        for b in range(4):
            backs += mm_nt(gb[:, b].reshape(64, H), wgu[b, KP:KE, :])
        sp[:, :, 0:EX] = mids.astype(BF).reshape(4, G, EX)
        sp[:, :, EX : 2 * EX] = backs.astype(BF).reshape(4, G, EX)
        for q in range(NX):
            send(sp.at[q], sa.at[x], sar.at[x], fid(q, z, c), y, own=lambda q=q: x == q)

    small_a()

    def small_b():
        for i in range(NX):
            wait(sa.at[i], sar.at[i])
        v = sa[0].astype(F32)
        for i in range(1, NX):
            v += sa[i].astype(F32)
        sb[...] = v.astype(BF)
        for dz in (4, 3, 5, 2, 6, 1, 7):
            send(sb, sc8.at[z], sc8r.at[z], fid(x, zp[dz], c), y)

    def small_c():
        v = sb[...].astype(F32)
        for dz in range(1, NZ):
            wait(sc8.at[zp[dz]], sc8r.at[zp[dz]])
            v += sc8[zp[dz]].astype(F32)
        sd[...] = v.astype(BF)
        for dx in (2, 1, 3):
            send(sd, se.at[x], ser.at[x], fid(xp[dx], z, c), y)

    def small_d():
        for dx in range(1, NX):
            wait(se.at[xp[dx]], ser.at[xp[dx]])
        se[x] = sd[...]
        for cc in range(2):
            lanes = pl.ds((1 - cc) * EX, EX)
            send(se.at[:, :, lanes], smm.at[blk], smr.at[blk], fid(x, z, cc), x,
                 own=lambda cc=cc: jnp.logical_and(c == cc, y == x))

    def small_e():
        for i in range(8):
            wait(smm.at[i], smr.at[i])
        small = jnp.concatenate(
            [smm[(zz // 4) * 4 + (xx + zz) % 4, zz % 4] for zz in range(NZ) for xx in range(NX)], axis=0
        )
        first = lax.div(z * 224, 128) * 128
        lead = z * 224 - first
        win = pl.ds(pl.multiple_of(first, 128), 384)
        res[...] = mm_tn(aa[:, :, :, win].reshape(512, 384), small)
        for cc in range(2):
            mb[cc, 0:112, :] = res[pl.ds(pl.multiple_of(lead + cc * 112, 8), 112), :].astype(BF)
        for dy in (2, 1, 3, 0):
            for cc in range(2):
                send(
                    mb.at[cc], fd.at[c], t3r.at[c], fid(x, z, cc), yp[dy],
                    own=(lambda cc=cc: c == cc) if dy == 0 else None,
                )
        drain(scope[-1], True)

    def order_ext():
        wait(ext, exr)
        for i in range(8):
            for q in range(4):
                zz = (i // 4) * 4 + q
                extp[(i * 4 + q) * G : (i * 4 + q + 1) * G, :] = ext[zz, (i % 4 + 8 - zz) % 4]

    def ring(d, slot, v, tgt):
        rss[d, slot] = v.astype(BF)
        send(rss.at[d, slot], rsr.at[d, slot], rsrs.at[d, slot], tgt, y)

    def come(d, slot):
        wait(rsr.at[d, slot], rsrs.at[d, slot])
        return rsr[d, slot].astype(F32)

    def total(n):
        v = xr[0].astype(F32)
        for i in range(1, n):
            v += xr[i].astype(F32)
        return v

    mycols = pl.ds(pl.multiple_of(y * KP, 128), KP)

    def finish(fin, back):
        mid = fin[:, KP:KE].astype(BF)
        fin = (fin[:, :KP] + mm(mid, back[:, mycols])).astype(BF)
        m = lax.broadcasted_iota(jnp.int32, (128, G), 0)
        r8 = lax.broadcasted_iota(jnp.int32, (128, G), 1) * 8
        acc = jnp.zeros((128, H), F32)
        for j in range(7):
            put = (m == r8 + j).astype(F32).astype(BF)
            acc += mm(put, fin[:, j * 256 : (j + 1) * 256])
        msg[...] = acc.astype(BF).reshape(8, G, H)

    def out0(ts):
        for t in ts:
            for yy in range(NY):
                i = lax.div(t, 4) * 4 + yy
                wait(hall.at[i, m4(t)], hallr.at[i * 4 + m4(t)])

        def rows(kb):
            return jnp.concatenate(
                [hall[lax.div(t, 4) * 4 + m4(t + xx), m4(t), kb] for t in ts for xx in range(NX)], axis=0
            )

        def body(nb, carry):
            cols = pl.ds(pl.multiple_of(nb * NB, 128), NB)
            po[0 : 64 * len(ts), cols] = mm(rows(0), wd[0, :, cols]) + mm(rows(1), wd[1, :, cols])
            return carry

        lax.fori_loop(0, KE // NB, body, 0)

    def scatter0():
        right, left = fid(x, zr, 0), fid(x, zl, 0)
        out0([zf])
        for xx in range(2):
            ring(0, xx, po[xx * G : (xx + 1) * G, :], right)
            ring(1, xx + 2, po[(xx + 2) * G : (xx + 3) * G, :], left)
        small_b()
        for s in range(1, 4):
            out0([zp[4 - s], zp[4 + s]])
            for xx in range(NX):
                v = po[xx * G : (xx + 1) * G, :]
                if s > 1 or xx < 2:
                    v = v + come(0, (s - 1) * 4 + xx)
                ring(0, s * 4 + xx, v, right)
                v = po[(4 + xx) * G : (5 + xx) * G, :]
                if s > 1 or xx >= 2:
                    v = v + come(1, (s - 1) * 4 + xx)
                ring(1, s * 4 + xx, v, left)
            if s == 1:
                small_c()
            if s == 2:
                small_d()
        out0([z])
        within("xy0", x == y, small_e)
        for xx in range(NX):
            v = po[xx * G : (xx + 1) * G, :] + come(0, 12 + xx) + come(1, 12 + xx)
            xs[xx] = v.astype(BF)
            send(xs.at[xx], xr.at[x], xrs.at[x], fid(xx, z, 0), y, own=lambda xx=xx: x == xx)
        order_ext()
        for b in range(2):
            dlp[b] = mm_tn(extp[...], hall[:, :, b].reshape(512, H))[0:R]
        send(dlp.at[1], dlr.at[0], lar.at[0], sib, y)
        for i in range(NX):
            wait(xr.at[i], xrs.at[i])
        finish(total(NX), dlv)

    def out1(t, dst):
        for zz in range(NZ):
            i = (zz // 4) * 4 + m4(t + zz)
            wait(gall.at[i, zz % 4], gallr.at[i * 4 + zz % 4])

        def rows(b):
            return jnp.concatenate(
                [gall[(zz // 4) * 4 + m4(t + zz), zz % 4, b] for zz in range(NZ)], axis=0
            )

        def body(nb, carry):
            cols = pl.ds(pl.multiple_of(nb * NB, 128), NB)
            acc = mm_nt(rows(0), wgu[0, cols, :])
            for b in range(1, 4):
                acc += mm_nt(rows(b), wgu[b, cols, :])
            dst[:, cols] = acc
            return carry

        lax.fori_loop(0, KE // NB, body, 0)

    def scatter1():
        right, left = fid(xrt, z, 1), fid(xlt, z, 1)
        out1(xf, po)
        for zz in range(4):
            ring(0, zz, po[zz * G : (zz + 1) * G, :], right)
            ring(1, zz + 4, po[(zz + 4) * G : (zz + 5) * G, :], left)
        small_b()
        out1(xrt, po)
        for zz in range(4, 8):
            ring(0, 8 + zz, po[zz * G : (zz + 1) * G, :], right)
        out1(xlt, pq)
        for zz in range(4):
            ring(1, 8 + zz, pq[zz * G : (zz + 1) * G, :], left)
        for zz in range(4):
            ring(0, 8 + zz, po[zz * G : (zz + 1) * G, :] + come(0, zz), right)
            ring(1, 12 + zz, pq[(zz + 4) * G : (zz + 5) * G, :] + come(1, zz + 4), left)
        small_c()
        out1(x, po)
        small_d()
        for zz in (4, 5, 6, 7, 0, 1, 2, 3):
            d0, d1 = come(0, 8 + zz), come(1, 8 + zz)
            xs[zz] = (po[zz * G : (zz + 1) * G, :] + d0 + d1).astype(BF)
            send(xs.at[zz], xr.at[z], xrs.at[z], fid(x, zz, 1), y, own=lambda zz=zz: z == zz)
        within("xy1", x == y, small_e)
        order_ext()
        for b in range(4):
            grad = mm_tn(extp[...], gall[:, :, b].reshape(512, H))
            dlp[b] = grad[0:R] if b < 2 else grad[R:EX]
        send(dlp.at[0], dlr.at[0], lar.at[0], sib, y)
        send(dlp.at[2], dlr.at[1], lar.at[1], sib, y)
        for i in range(NZ):
            wait(xr.at[i], xrs.at[i])
        finish(total(NZ), gev)

    within(0, c == 0, scatter0)
    within(1, c == 1, scatter1)

    for dy in (2, 1, 3, 0):
        for cc in range(2):
            send(
                msg.at[yp[dy] * 2 + cc], rowsr.at[c, y], rowss.at[c, y],
                fid(x, z, cc), yp[dy], own=(lambda cc=cc: c == cc) if dy == 0 else None,
            )

    @pl.when(c == 0)
    def _():
        wait(dlr.at[0], lar.at[0])
        wait(dlr.at[1], lar.at[1])
        dla_out[0] = dlp[0]
        dla_out[1] = dlr[0]
        dla_out[2] = dlr[1]

    @pl.when(c == 1)
    def _():
        wait(dlr.at[0], lar.at[0])
        dla_out[0] = dlr[0]
        dla_out[1] = dlp[1]
        dla_out[2] = dlp[3]

    wait(fd.at[0], t3r.at[0])
    wait(fd.at[1], t3r.at[1])
    fd_out[...] = fd[...].astype(F32)
    for k in range(2):
        for s in range(NY):
            wait(rowsr.at[k, s], rowss.at[k, s])
    rows_out[...] = rowsr[...].astype(F32)
    for name in scopes:
        drain(name)


def place(rows_ref, fd_ref, dla_ref, lo, gt, dget, dgl, duet, dul, ddet, ddl, row):
    for kind, ref in enumerate((lo, gt)):
        for yy in range(NY):
            for t in range(2):
                for j in range(7):
                    row[t : t + 1, yy * KP + j * 256 : yy * KP + (j + 1) * 256] = rows_ref[
                        kind, yy, t * 8 + j : t * 8 + j + 1, :
                    ]
        ref[...] = row[...].astype(BF)
    v = fd_ref[0].T
    dget[...] = v[:R, :112]
    duet[...] = v[R:EX, :112]
    ddl[...] = fd_ref[1].T[:R, :112]
    ddet[...] = dla_ref[0]
    dgl[...] = dla_ref[1]
    dul[...] = dla_ref[2]


def dma(*shape):
    return pltpu.SemaphoreType.DMA(shape)


def on_device(
    tokens, grad_out, gate_codes, gate_scales, up_codes, up_scales, down_codes, down_scales,
    gate_enter, gate_leave, up_enter, up_leave, down_enter, down_leave,
):
    scales = jnp.concatenate([gate_scales.T, up_scales.T, down_scales], axis=0).astype(F32)
    vm = pl.BlockSpec(memory_space=pltpu.VMEM)
    sm = pl.BlockSpec(memory_space=pltpu.SMEM)
    hb = pl.BlockSpec(memory_space=pltpu.HBM)
    V = pltpu.VMEM
    one = pltpu.SemaphoreType.DMA
    scratch = [
        V((KP, H), BF), V((KP, H), BF), V((H, KP), BF), V((EX, NY * KP), BF), V((EX, NY * KP), BF), dma(6),
        V((2, NY, G, H), F32), V((2, NY, G, H), BF), V((8, G, H), BF), dma(8),
        V((4, KE, H), BF), V((2, H, KE), BF), dma(3),
        V((NZ, NX, G, KE), BF), dma(32),
        V((NZ, NX, G, EX), BF), V((512, EX), BF), one,
        V((NZ, NX, 4, G, H), BF), V((NY, 4, 4, G, H), BF), dma(16),
        V((NX, NZ, 2, G, H), BF), V((NY, 4, 2, G, H), BF), dma(16),
        V((4, 2, G, H), BF), V((8, 4, 2, G, H), BF), dma(32),
        V((4, 4, G, H), BF), V((8, 4, 4, G, H), BF), dma(32),
        V((128, KE), F32), V((128, KE), F32), V((2, 16, G, KE), BF), V((2, 16, G, KE), BF), dma(2, 16),
        V((8, G, KE), BF), V((8, G, KE), BF), dma(8),
        V((8, G, H), BF), V((2, NY, G, H), BF), dma(2, NY),
        V((4, G, H), BF), V((NX, G, H), BF), dma(NX), V((G, H), BF), V((NZ, G, H), BF), dma(NZ),
        V((G, H), BF), V((NX, G, H), BF), dma(NX), V((8, 4, G, EX), BF), dma(8),
        V((384, EX), F32), V((2, EX, EX), BF), V((2, EX, EX), BF), dma(2),
        V((4, R, H), F32), V((2, R, H), F32), dma(2),
        dma(55), dma(111), dma(8),
    ]
    S = jax.ShapeDtypeStruct
    rows, fd, dla = pl.pallas_call(
        kernel,
        out_shape=[S((2, NY, G, H), F32), S((2, EX, EX), F32), S((3, R, H), F32)],
        in_specs=[vm, vm, sm, hb, hb, hb, vm, vm, vm, hb, hb, hb],
        out_specs=[vm] * 3,
        scratch_shapes=scratch,
        compiler_params=pltpu.CompilerParams(
            collective_id=0, has_side_effects=True, vmem_limit_bytes=63 * 1024 * 1024
        ),
        name="lora_ffn_step",
    )(
        tokens, grad_out, scales, gate_codes, up_codes, down_codes, gate_leave, up_leave, down_enter.T,
        gate_enter.T, up_enter.T, down_leave,
    )
    lo, gt, dget, dgl, duet, dul, ddet, ddl = pl.pallas_call(
        place,
        out_shape=[
            S((2, NY * KP), BF), S((2, NY * KP), BF), S((R, 112), F32), S((R, H), F32),
            S((R, 112), F32), S((R, H), F32), S((R, H), F32), S((R, 112), F32),
        ],
        in_specs=[vm] * 3,
        out_specs=[vm] * 8,
        scratch_shapes=[V((2, NY * KP), F32)],
        name="place_outputs",
    )(rows, fd, dla)
    return lo, gt, dget.T, dgl, duet.T, dul, ddet.T, ddl


def solution(mesh):
    return jax.shard_map(
        on_device,
        mesh=mesh,
        in_specs=(
            P(("fsdp", "dp"), None),
            P(("fsdp", "dp"), None),
            P("dp", "fsdp"),
            P("dp", "fsdp"),
            P("dp", "fsdp"),
            P("dp", "fsdp"),
            P("fsdp", "dp"),
            P("fsdp", "dp"),
            P(),
            P(None, "fsdp"),
            P(),
            P(None, "fsdp"),
            P("fsdp", None),
            P(),
        ),
        out_specs=(
            P(("fsdp", "dp"), None),
            P(("fsdp", "dp"), None),
            P("fsdp", None),
            P(None, "fsdp"),
            P("fsdp", None),
            P(None, "fsdp"),
            P("fsdp", None),
            P(None, "fsdp"),
        ),
        check_vma=False,
    )
```

```python
import jax
import jax.numpy as jnp
from jax import lax
from jax.experimental import pallas as pl
from jax.experimental.pallas import tpu as pltpu
from jax.sharding import PartitionSpec as P

NX, NZ, NY = 4, 8, 4
KP, KE, EX = 1792, 1920, 128
G, H, R = 16, 256, 64
NB = 384
BF, F32 = jnp.bfloat16, jnp.float32
MESH = pl.DeviceIdType.MESH


def mm(a, b):
    return jnp.dot(a, b, preferred_element_type=F32)


def mm_nt(a, b):
    return lax.dot_general(a, b, (((1,), (1,)), ((), ())), preferred_element_type=F32)


def mm_tn(a, b):
    return lax.dot_general(a, b, (((0,), (0,)), ((), ())), preferred_element_type=F32)


def kernel(
    tok_hbm, gout_hbm, gs_hbm, us_hbm, ds_hbm, gc_hbm, uc_hbm, dc_hbm, gl_hbm, ul_hbm, det_hbm, get_hbm, uet_hbm, dl_hbm,
    rows_out, fd_out, dla_out,
    tokv, goutv, scv, detv, gcv, ucv, dcv, gev, dlv, ldsem, zsem,
    sf, sends, st1, s1r,
    wgu, wd, wsr,
    aa, agr,
    ext, extp, exr,
    part, rgu, gur,
    parth, rh, hr,
    hb, hall, hallr,
    gb, gall,
    po, pq, rss, rsr, rsrs,
    msg, rows0, rows1, rowss, rowsf, outsem, gota, gotb,
    sp, sa, sar, sb, sc8, sc8r, sd, se, ser, smm, smr,
    res, mb, fd, t3r,
    dlp, dlr, lar,
    gsem,
):
    f = lax.axis_index("fsdp")
    y = lax.axis_index("dp")
    x = lax.div(f, 16)
    z = lax.rem(lax.div(f, 2), 8)
    c = lax.rem(f, 2)
    o = 1 - c

    def fid(xx, zz, cc):
        return xx * 16 + zz * 2 + cc

    def m4(v):
        return lax.rem(v, 4)

    def m8(v):
        return lax.rem(v, 8)

    zp = [m8(z + k) for k in range(NZ)]
    xp = [m4(x + k) for k in range(NX)]
    yp = [m4(y + k) for k in range(NY)]

    def rcopy(src, dst, ssem, rsem, ff, yy):
        return pltpu.make_async_remote_copy(
            src_ref=src, dst_ref=dst, send_sem=ssem, recv_sem=rsem,
            device_id={"fsdp": ff, "dp": yy}, device_id_type=MESH,
        )

    def wait(ref, sem):
        pltpu.make_async_copy(ref, ref, sem).wait()

    def send(src, dst, kind, rsem, ff, yy, own=None):
        ssem = gsem.at[kind]
        if own is None:
            rcopy(src, dst, ssem, rsem, ff, yy).start()
            return

        @pl.when(own)
        def _():
            pltpu.make_async_copy(src, dst, rsem).start()

        @pl.when(jnp.logical_not(own))
        def _():
            rcopy(src, dst, ssem, rsem, ff, yy).start()

    def sent(kind, ref):
        wait(ref, gsem.at[kind])

    loads = [
        pltpu.make_async_copy(get_hbm, gev.at[pl.ds(0, R)], ldsem.at[0]),
        pltpu.make_async_copy(uet_hbm, gev.at[pl.ds(R, R)], ldsem.at[1]),
        pltpu.make_async_copy(dl_hbm, dlv.at[pl.ds(0, R)], ldsem.at[2]),
        pltpu.make_async_copy(gc_hbm, gcv, ldsem.at[3]),
        pltpu.make_async_copy(uc_hbm, ucv, ldsem.at[4]),
        pltpu.make_async_copy(dc_hbm, dcv, ldsem.at[5]),
        pltpu.make_async_copy(tok_hbm, tokv, ldsem.at[6]),
        pltpu.make_async_copy(gout_hbm, goutv, ldsem.at[7]),
        pltpu.make_async_copy(gs_hbm, scv.at[0], ldsem.at[8]),
        pltpu.make_async_copy(gl_hbm, wgu.at[c, pl.ds(KP, R)], ldsem.at[9]),
        pltpu.make_async_copy(ul_hbm, wgu.at[2 + c, pl.ds(KP + R, R)], ldsem.at[10]),
        pltpu.make_async_copy(det_hbm, detv, ldsem.at[11]),
        pltpu.make_async_copy(us_hbm, scv.at[1], ldsem.at[12]),
        pltpu.make_async_copy(ds_hbm, scv.at[2], ldsem.at[13]),
    ]
    for i in (6, 7, 0, 1, 2, 8, 12, 13, 9, 3, 10, 4, 11, 5):
        loads[i].start()

    barrier = pltpu.get_barrier_semaphore()
    peers = []
    for dx in range(NX):
        for dy in range(NY):
            for dc in range(2):
                if dx or dy or dc:
                    peers.append((fid(xp[dx], z, lax.rem(c + dc, 2)), yp[dy]))
    for dz in range(1, NZ):
        peers.append((fid(x, zp[dz], c), y))
    for ff, yy in peers:
        pl.semaphore_signal(barrier, inc=1, device_id={"fsdp": ff, "dp": yy}, device_id_type=MESH)

    dlv[R:EX, :] = jnp.zeros((R, NY * KP), BF)
    for kind, ref in enumerate((tokv, goutv)):
        loads[6 + kind].wait()
        v = ref[...].astype(F32)
        v16 = jnp.concatenate([v, jnp.zeros((14, NY * KP), F32)], axis=0).astype(BF)
        for yy in range(NY):
            for t in range(2):
                for j in range(7):
                    sf[kind, yy, t * 8 + j : t * 8 + j + 1, :] = v[
                        t : t + 1, yy * KP + j * 256 : yy * KP + (j + 1) * 256
                    ]
        if kind == 0:
            loads[0].wait()
            loads[1].wait()
            e = mm_nt(v16, gev[...])
        else:
            loads[2].wait()
            e = mm_nt(v16, dlv[...])
        for yy in range(NY):
            for t in range(2):
                sf[kind, yy, t * 8 + 7 : t * 8 + 8, :] = jnp.concatenate(
                    [e[t : t + 1], jnp.zeros((1, EX), F32)], axis=1
                )
    sends[...] = sf[...].astype(BF)
    pl.semaphore_wait(barrier, len(peers))

    for dz in range(1, NZ):
        pl.semaphore_signal(
            zsem, inc=1, device_id={"fsdp": fid(x, zp[dz], c), "dp": y}, device_id_type=MESH
        )

    src1 = y * 2 + c
    for dx in (2, 1, 3, 0):
        for dy in (2, 1, 3, 0):
            send(
                sends.at[0, yp[dy]], st1.at[x, src1], 0, s1r.at[x], fid(xp[dx], z, 0), yp[dy],
                own=(c == 0) if dx == 0 and dy == 0 else None,
            )
            if dx == 0:
                send(
                    sends.at[1, yp[dy]], st1.at[x, src1], 0, s1r.at[x], fid(x, z, 1), yp[dy],
                    own=(c == 1) if dy == 0 else None,
                )

    def scale(k, i):
        lane = lax.broadcasted_iota(jnp.int32, (2, 14), 1)
        return jnp.sum(jnp.where(lane == i, scv[k].astype(F32), 0.0), axis=1, keepdims=True)

    def dequant_cols(codes, slot, k):
        def body(i, carry):
            rows = pl.ds(pl.multiple_of(i * 128, 128), 128)
            v = scale(k, i)
            wgu[slot, rows, 0:128] = (codes[rows, 0:128].astype(F32) * v[0:1]).astype(BF)
            wgu[slot, rows, 128:256] = (codes[rows, 128:256].astype(F32) * v[1:2]).astype(BF)
            return carry

        lax.fori_loop(0, 14, body, 0)

    sib = fid(x, z, o)
    for i in (8, 12, 13):
        loads[i].wait()
    loads[3].wait()
    dequant_cols(gcv, c, 0)
    loads[9].wait()
    wgu[c, KP + R :, :] = jnp.zeros((R, H), BF)
    send(wgu.at[c], wgu.at[c], 1, wsr.at[0], sib, y)
    loads[4].wait()
    dequant_cols(ucv, 2 + c, 1)
    wgu[2 + c, KP : KP + R, :] = jnp.zeros((R, H), BF)
    loads[10].wait()
    send(wgu.at[2 + c], wgu.at[2 + c], 2, wsr.at[1], sib, y)
    loads[5].wait()
    loads[11].wait()

    def dequant_down(i, carry):
        cols = pl.ds(pl.multiple_of(i * 128, 128), 128)
        v = scale(2, i)
        wd[c, 0:128, cols] = (dcv[0:128, cols].astype(F32) * v[0:1]).astype(BF)
        wd[c, 128:256, cols] = (dcv[128:256, cols].astype(F32) * v[1:2]).astype(BF)
        return carry

    lax.fori_loop(0, 14, dequant_down, 0)
    det = jnp.concatenate([detv[...].astype(F32), jnp.zeros((R, H), F32)], axis=0)
    wd[c, :, KP:KE] = det.T.astype(BF)
    send(wd.at[c], wd.at[c], 3, wsr.at[2], sib, y)

    def unpack(xx):
        wait(st1.at[xx], s1r.at[xx])
        got = st1[xx].reshape(128, H).astype(F32)
        for h, part_ref in enumerate((gota, gotb)):
            part_ref[...] = got[:, h * 128 : (h + 1) * 128]
            for j in range(8 - h):
                k = 2 * j + h
                aa[z, xx, :, k * 128 : (k + 1) * 128] = part_ref[pl.ds(j, G, stride=8), :].astype(BF)

    flag = jnp.where(y == 0, 1.0, 0.0).astype(F32)

    def masked(v):
        return (v.astype(F32) * flag).astype(BF)

    def have(zz, xx):
        wait(aa.at[zz, xx], agr.at[zz * 4 + xx])

    def fwd(zz, xx, tz, tx):
        send(aa.at[zz, xx], aa.at[zz, xx], 4, agr.at[zz * 4 + xx], fid(tx, tz, c), y)

    zr, zl, zf = zp[1], zp[7], zp[4]
    xrt, xlt, xf = xp[1], xp[3], xp[2]

    def weights():
        wait(wgu.at[o], wsr.at[0])
        wait(wgu.at[2 + o], wsr.at[1])
        wait(wd.at[o], wsr.at[2])

    def front0(zs):
        def body(b, carry):
            a = jnp.concatenate([aa[zz].reshape(64, KE) for zz in zs], axis=0)
            acc = mm(a[:, :KP], wgu[b, 0:KP, :]) + mm(masked(a[:, KP:]), wgu[b, KP:KE, :])
            acc = acc.astype(BF)
            for i, zz in enumerate(zs):
                part[zz, :, b] = acc[i * 64 : (i + 1) * 64].reshape(4, G, H)
            return carry

        lax.fori_loop(0, 4, body, 0)
        for zz in zs:
            for xx in range(NX):
                send(
                    part.at[zz, xx], rgu.at[y, m4(zz)], 6, gur.at[m4(zz)],
                    fid(x, z, lax.div(zz, 4)), m4(zz + xx),
                    own=jnp.logical_and(m4(zz + xx) == y, zz < 4),
                )

    def front1(xx):
        def body(b, carry):
            a = aa[:, xx].reshape(128, KE)
            acc = mm_nt(a[:, :KP], wd[b, :, 0:KP]) + mm_nt(masked(a[:, KP:]), wd[b, :, KP:KE])
            parth[xx, :, b] = acc.astype(BF).reshape(8, G, H)
            return carry

        lax.fori_loop(0, 2, body, 0)
        for zz in range(NZ):
            send(
                parth.at[xx, zz], rh.at[y, zz % 4], 6, hr.at[zz % 4],
                fid(x, z, zz // 4), m4(xx + zz), own=(m4(xx + zz) == y) if zz >= 4 else None,
            )

    def gather0():
        for xx in (x, xrt, xlt, xf):
            unpack(xx)
            fwd(z, xx, zr, x)
            fwd(z, xx, zl, x)
        weights()
        front0([z])
        for k in range(1, 4):
            za, zb = zp[8 - k], zp[k]
            for i, xx in enumerate((x, xrt, xlt, xf)):
                have(za, xx)
                if k < 3 or i < 1:
                    fwd(za, xx, zr, x)
                have(zb, xx)
                if k < 3 or i >= 1:
                    fwd(zb, xx, zl, x)
            front0([za, zb])
        for xx in range(NX):
            have(zf, xx)
        send(aa.at[:, :, :, pl.ds(KP, EX)], ext, 5, exr, sib, y)
        front0([zf])

    def gather1():
        unpack(x)
        for dz in (1, 7, 2, 6):
            fwd(z, x, zp[dz], x)

        def spread(zz, far=False):
            fwd(zz, x, z, xrt)
            fwd(zz, x, z, xlt)
            if far:
                fwd(zz, x, z, xf)

        def xstep(dz):
            have(zp[dz], xrt)
            fwd(zp[dz], xrt, z, xlt)

        spread(z)
        have(zp[7], x)
        spread(zp[7])
        have(zp[1], x)
        spread(zp[1])
        have(zp[6], x)
        fwd(zp[6], x, zr, x)
        fwd(zp[6], x, zp[2], x)
        have(zp[2], x)
        fwd(zp[2], x, zl, x)
        spread(zp[6])
        spread(zp[2])
        xstep(0)
        xstep(7)
        xstep(1)
        for dz in (5, 3, 4):
            have(zp[dz], x)
            spread(zp[dz], True)
        xstep(6)
        xstep(2)
        weights()
        front1(x)
        for dz in (3, 4, 5):
            have(zp[dz], xrt)
        front1(xrt)
        for dz in range(NZ):
            have(zp[dz], xlt)
        front1(xlt)
        for dz in range(NZ):
            have(zp[dz], xf)
        send(aa.at[:, :, :, pl.ds(KP, EX)], ext, 5, exr, sib, y)
        front1(xf)

    pl.when(c == 0)(gather0)
    pl.when(c == 1)(gather1)

    def middle(q, carry):
        wait(rgu.at[:, q], gur.at[q])
        wait(rh.at[:, q], hr.at[q])
        for b in range(2):
            g = rgu[0, q, b].astype(F32)
            u = rgu[0, q, 2 + b].astype(F32)
            h = rh[0, q, b].astype(F32)
            for s in range(1, NY):
                g += rgu[s, q, b].astype(F32)
                u += rgu[s, q, 2 + b].astype(F32)
                h += rh[s, q, b].astype(F32)
            sig = jax.nn.sigmoid(g)
            act = g * sig
            hb[q, b] = (act * u).astype(BF)
            gb[q, b] = (h * u * sig * (1.0 + g * (1.0 - sig))).astype(BF)
            gb[q, 2 + b] = (h * act).astype(BF)
        return carry

    lax.fori_loop(0, 4, middle, 0)
    blk = c * 4 + y
    for i in range(4):
        qh = m4(z + (0, 3, 1, 2)[i])
        qg = m4(y + 8 - x - (2, 1, 3, 0)[i])
        for dy in (2, 1, 3, 0):
            send(gb.at[qg], gall.at[blk, qg], 7, hallr.at[m4(y + 4 - qg)], fid(x, z, 1), yp[dy],
                 own=(c == 1) if dy == 0 else None)
            send(hb.at[qh], hall.at[blk, qh], 8, hallr.at[c * 4 + qh], fid(x, z, 0), yp[dy],
                 own=(c == 0) if dy == 0 else None)

    def small_a():
        mids = jnp.zeros((64, EX), F32)
        backs = jnp.zeros((64, EX), F32)
        for b in range(2):
            mids += mm(hb[:, b].reshape(64, H), wd[b, :, KP:KE])
        for b in range(4):
            backs += mm_nt(gb[:, b].reshape(64, H), wgu[b, KP:KE, :])
        sp[:, :, 0:EX] = mids.astype(BF).reshape(4, G, EX)
        sp[:, :, EX : 2 * EX] = backs.astype(BF).reshape(4, G, EX)
        for q in range(NX):
            send(sp.at[q], sa.at[x], 9, sar, fid(q, z, c), y, own=x == q)

    def small_b():
        wait(sa, sar)
        v = sa[0].astype(F32)
        for i in range(1, NX):
            v += sa[i].astype(F32)
        sb[...] = v.astype(BF)
        for dz in (4, 3, 5, 2, 6, 1, 7):
            send(sb, sc8.at[z], 10, sc8r, fid(x, zp[dz], c), y)

    def small_c():
        v = sb[...].astype(F32)
        wait(sc8.at[pl.ds(0, NZ - 1)], sc8r)
        for dz in range(1, NZ):
            v += sc8[zp[dz]].astype(F32)
        sd[...] = v.astype(BF)
        for dx in (2, 1, 3):
            send(sd, se.at[x], 11, ser, fid(xp[dx], z, c), y)

    def small_d():
        wait(se.at[pl.ds(0, NX - 1)], ser)
        se[x] = sd[...]
        for cc in range(2):
            lanes = pl.ds((1 - cc) * EX, EX)
            send(se.at[:, :, lanes], smm.at[blk], 12 + cc, smr, fid(x, z, cc), x,
                 own=jnp.logical_and(c == cc, y == x))

    def small_e():
        wait(smm, smr)
        small = jnp.concatenate(
            [smm[(zz // 4) * 4 + (xx + zz) % 4, zz % 4] for zz in range(NZ) for xx in range(NX)], axis=0
        )
        first = lax.div(z * 224, 128) * 128
        lead = z * 224 - first
        win = pl.ds(pl.multiple_of(first, 128), 384)
        res[...] = mm_tn(aa[:, :, :, win].reshape(512, 384), small)
        for cc in range(2):
            mb[cc, 0:112, :] = res[pl.ds(pl.multiple_of(lead + cc * 112, 8), 112), :].astype(BF)
        for dy in (2, 1, 3, 0):
            for cc in range(2):
                send(
                    mb.at[cc], fd.at[c], 17, t3r.at[c], fid(x, z, cc), yp[dy],
                    own=(c == cc) if dy == 0 else None,
                )
        sent(17, part.at[pl.ds(0, 7), 0])

    def order_ext():
        wait(ext, exr)
        for i in range(8):
            for q in range(4):
                zz = (i // 4) * 4 + q
                extp[(i * 4 + q) * G : (i * 4 + q + 1) * G, :] = ext[zz, (i % 4 + 8 - zz) % 4]

    def ring(d, slot, v, tgt):
        k = d * 16 + slot
        rss[k] = v.astype(BF)
        send(rss.at[k], rsr.at[k], 14, rsrs.at[k], tgt, y)

    def come(d, slot):
        k = d * 16 + slot
        wait(rsr.at[k], rsrs.at[k])
        return rsr[k].astype(F32)

    mycols = pl.ds(pl.multiple_of(y * KP, 128), KP)

    def last(g, v, back, xx, zz, here, rows, rsem, slot):
        v = v[:, :KP] + mm(v[:, KP:KE].astype(BF), back[:, mycols])
        for j in range(7):
            gota[pl.ds(j, G, stride=8), :] = v[:, j * 256 : j * 256 + 128]
            gotb[pl.ds(j, G, stride=8), :] = v[:, j * 256 + 128 : (j + 1) * 256]
        msg[g * 8 : (g + 1) * 8, :, 0:128] = gota[...].astype(BF).reshape(8, G, 128)
        msg[g * 8 : (g + 1) * 8, :, 128:256] = gotb[...].astype(BF).reshape(8, G, 128)
        for dy in (2, 1, 3, 0):
            for cc in range(2):
                send(
                    msg.at[g * 8 + yp[dy] * 2 + cc], rows.at[slot, y], 16, rsem, fid(xx, zz, cc), yp[dy],
                    own=jnp.logical_and(c == cc, here) if dy == 0 else None,
                )

    def out0(ts):
        for t in ts:
            wait(hall.at[pl.ds(lax.div(t, 4) * 4, 4), m4(t)], hallr.at[t])

        def rows(kb):
            return jnp.concatenate(
                [hall[lax.div(t, 4) * 4 + m4(t + xx), m4(t), kb] for t in ts for xx in range(NX)], axis=0
            )

        def body(nb, carry):
            cols = pl.ds(pl.multiple_of(nb * NB, 128), NB)
            po[0 : 64 * len(ts), cols] = mm(rows(0), wd[0, :, cols]) + mm(rows(1), wd[1, :, cols])
            return carry

        lax.fori_loop(0, KE // NB, body, 0)

    def scatter0():
        right, left = fid(x, zr, 0), fid(x, zl, 0)
        out0([zf])
        for xx in range(2):
            ring(0, xx, po[xx * G : (xx + 1) * G, :], right)
            ring(1, xx + 2, po[(xx + 2) * G : (xx + 3) * G, :], left)
        small_a()
        pl.semaphore_wait(zsem, NZ - 1)
        for s in range(1, 4):
            out0([zp[4 - s], zp[4 + s]])
            for xx in range(NX):
                v = po[xx * G : (xx + 1) * G, :]
                if s > 1 or xx < 2:
                    v = v + come(0, (s - 1) * 4 + xx)
                ring(0, s * 4 + xx, v, right)
                v = po[(4 + xx) * G : (5 + xx) * G, :]
                if s > 1 or xx >= 2:
                    v = v + come(1, (s - 1) * 4 + xx)
                ring(1, s * 4 + xx, v, left)
            (small_b, small_c, small_d)[s - 1]()
        out0([z])
        for xx in range(NX):
            v = po[xx * G : (xx + 1) * G, :] + come(0, 12 + xx) + come(1, 12 + xx)
            last(xx, v, dlv, xx, z, x == xx, rows0, rowss.at[0], x)
        order_ext()
        for b in range(2):
            dlp[b] = mm_tn(extp[...], hall[:, :, b].reshape(512, H))[0:R]
        send(dlp.at[1], dlr.at[0], 15, lar.at[0], sib, y)
        pl.when(x == y)(small_e)
        sent(4, rsr.at[pl.ds(0, 28)])
        sent(6, part.at[pl.ds(0, 7)])
        sent(7, part.at[pl.ds(0, 4)])
        sent(8, part.at[pl.ds(0, 3), pl.ds(0, 2)])
        sent(14, rsr.at[pl.ds(0, 28)])
        sent(15, dlp.at[0])
        sent(16, msg.at[pl.ds(0, 31)])

    def out1(t, dst):
        wait(gall.at[:, 0], hallr.at[t])

        def rows(b):
            return jnp.concatenate(
                [gall[(zz // 4) * 4 + m4(t + zz), zz % 4, b] for zz in range(NZ)], axis=0
            )

        def body(nb, carry):
            cols = pl.ds(pl.multiple_of(nb * NB, 128), NB)
            acc = mm_nt(rows(0), wgu[0, cols, :])
            for b in range(1, 4):
                acc += mm_nt(rows(b), wgu[b, cols, :])
            dst[:, cols] = acc
            return carry

        lax.fori_loop(0, KE // NB, body, 0)

    def scatter1():
        right, left = fid(xrt, z, 1), fid(xlt, z, 1)
        out1(xf, po)
        for zz in range(4):
            ring(0, zz, po[zz * G : (zz + 1) * G, :], right)
            ring(1, zz + 4, po[(zz + 4) * G : (zz + 5) * G, :], left)
        small_a()
        pl.semaphore_wait(zsem, NZ - 1)
        out1(xrt, po)
        for zz in range(4, 8):
            ring(0, 8 + zz, po[zz * G : (zz + 1) * G, :], right)
        out1(xlt, pq)
        for zz in range(4):
            ring(1, 8 + zz, pq[zz * G : (zz + 1) * G, :], left)
        for zz in range(4):
            ring(0, 8 + zz, po[zz * G : (zz + 1) * G, :] + come(0, zz), right)
            ring(1, 12 + zz, pq[(zz + 4) * G : (zz + 5) * G, :] + come(1, zz + 4), left)
        small_b()
        out1(x, po)
        small_c()
        for zz in (0, 4, 1, 5, 2, 6, 3, 7):
            v = po[zz * G : (zz + 1) * G, :] + come(0, 8 + zz) + come(1, 8 + zz)
            last(zz, v, gev, x, zz, z == zz, rows1, rowss.at[1], z)
        small_d()
        order_ext()
        for b in range(4):
            grad = mm_tn(extp[...], gall[:, :, b].reshape(512, H))
            dlp[b] = grad[0:R] if b < 2 else grad[R:EX]
        send(dlp.at[0], dlr.at[0], 15, lar.at[0], sib, y)
        send(dlp.at[2], dlr.at[1], 15, lar.at[1], sib, y)
        pl.when(x == y)(small_e)
        sent(4, rsr.at[pl.ds(0, 31)])
        sent(6, part.at[pl.ds(0, 7), pl.ds(0, 2)])
        sent(7, part.at[pl.ds(0, 3)])
        sent(8, part.at[pl.ds(0, 2)])
        sent(14, rsr.at[pl.ds(0, 24)])
        sent(15, dlp.at[pl.ds(0, 2)])
        sent(16, msg.at[pl.ds(0, 63)])

    pl.when(c == 0)(scatter0)
    pl.when(c == 1)(scatter1)

    def give(pairs):
        for i, (ref, sem) in enumerate(pairs):
            if sem is not None:
                wait(ref, sem)
            pltpu.make_async_copy(ref, dla_out.at[i], outsem.at[i]).start()

    pl.when(c == 0)(lambda: give(((dlp.at[0], None), (dlr.at[0], lar.at[0]), (dlr.at[1], lar.at[1]))))
    pl.when(c == 1)(lambda: give(((dlr.at[0], lar.at[0]), (dlp.at[1], None), (dlp.at[3], None))))
    wait(fd.at[0], t3r.at[0])
    wait(fd.at[1], t3r.at[1])
    out_fd = pltpu.make_async_copy(fd, fd_out, outsem.at[3])
    out_fd.start()
    for kind, (rows, n) in enumerate(((rows0, NX), (rows1, NZ))):
        wait(rows, rowss.at[kind])
        v = rows[0].astype(F32)
        for i in range(1, n):
            v += rows[i].astype(F32)
        rowsf[kind] = v
    out_rows = pltpu.make_async_copy(rowsf, rows_out, outsem.at[4])
    out_rows.start()
    for i in range(3):
        wait(dlp.at[0], outsem.at[i])
    out_fd.wait()
    out_rows.wait()
    sent(0, msg.at[pl.ds(0, 19)])
    sent(1, wgu.at[0])
    sent(2, wgu.at[0])
    sent(3, wd.at[0])
    sent(5, ext)
    sent(9, msg.at[pl.ds(0, 3)])
    sent(10, msg.at[pl.ds(0, 7)])
    sent(11, msg.at[pl.ds(0, 3)])
    for cc in range(2):
        @pl.when(jnp.logical_not(jnp.logical_and(c == cc, y == x)))
        def _(cc=cc):
            sent(12 + cc, smm.at[0])


def place(rows_ref, fd_ref, dla_ref, lo, gt, dget, dgl, duet, dul, ddet, ddl, row):
    for kind, ref in enumerate((lo, gt)):
        for yy in range(NY):
            for t in range(2):
                for j in range(7):
                    row[t : t + 1, yy * KP + j * 256 : yy * KP + (j + 1) * 256] = rows_ref[
                        kind, yy, t * 8 + j : t * 8 + j + 1, :
                    ]
        ref[...] = row[...].astype(BF)
    v = fd_ref[0].astype(F32).T
    dget[...] = v[:R, :112]
    duet[...] = v[R:EX, :112]
    ddl[...] = fd_ref[1].astype(F32).T[:R, :112]
    ddet[...] = dla_ref[0]
    dgl[...] = dla_ref[1]
    dul[...] = dla_ref[2]


def dma(*shape):
    return pltpu.SemaphoreType.DMA(shape)


def on_device(
    tokens, grad_out, gate_codes, gate_scales, up_codes, up_scales, down_codes, down_scales,
    gate_enter, gate_leave, up_enter, up_leave, down_enter, down_leave,
):
    vm = pl.BlockSpec(memory_space=pltpu.VMEM)
    hb = pl.BlockSpec(memory_space=pltpu.HBM)
    V = pltpu.VMEM
    one = pltpu.SemaphoreType.DMA
    scratch = [
        V((2, NY * KP), BF), V((2, NY * KP), BF), V((3, 2, 14), BF), V((R, H), BF),
        V((KP, H), BF), V((KP, H), BF), V((H, KP), BF), V((EX, NY * KP), BF), V((EX, NY * KP), BF), dma(14),
        pltpu.SemaphoreType.REGULAR,
        V((2, NY, G, H), F32), V((2, NY, G, H), BF), V((NX, 8, G, H), BF), dma(NX),
        V((4, KE, H), BF), V((2, H, KE), BF), dma(3),
        V((NZ, NX, G, KE), BF), dma(32),
        V((NZ, NX, G, EX), BF), V((512, EX), BF), one,
        V((NZ, NX, 4, G, H), BF), V((NY, 4, 4, G, H), BF), dma(4),
        V((NX, NZ, 2, G, H), BF), V((NY, 4, 2, G, H), BF), dma(4),
        V((4, 2, G, H), BF), V((8, 4, 2, G, H), BF), dma(8),
        V((4, 4, G, H), BF), V((8, 4, 4, G, H), BF),
        V((128, KE), F32), V((128, KE), F32), V((32, G, KE), BF), V((32, G, KE), BF), dma(32),
        V((64, G, H), BF), V((NX, NY, G, H), BF), V((NZ, NY, G, H), BF), dma(2),
        V((2, NY, G, H), F32), dma(5), V((128, 128), F32), V((128, 128), F32),
        V((4, G, H), BF), V((NX, G, H), BF), one, V((G, H), BF), V((NZ, G, H), BF), one,
        V((G, H), BF), V((NX, G, H), BF), one, V((8, 4, G, EX), BF), one,
        V((384, EX), F32), V((2, EX, EX), BF), V((2, EX, EX), BF), dma(2),
        V((4, R, H), F32), V((2, R, H), F32), dma(2),
        dma(18),
    ]
    S = jax.ShapeDtypeStruct
    rows, fd, dla = pl.pallas_call(
        kernel,
        out_shape=[S((2, NY, G, H), F32), S((2, EX, EX), BF), S((3, R, H), F32)],
        in_specs=[hb] * 14,
        out_specs=[hb] * 3,
        scratch_shapes=scratch,
        compiler_params=pltpu.CompilerParams(
            collective_id=0, has_side_effects=True, vmem_limit_bytes=63 * 1024 * 1024
        ),
        name="lora_ffn_step",
    )(
        tokens, grad_out, gate_scales.T, up_scales.T, down_scales, gate_codes, up_codes, down_codes, gate_leave, up_leave, down_enter.T,
        gate_enter.T, up_enter.T, down_leave,
    )
    lo, gt, dget, dgl, duet, dul, ddet, ddl = pl.pallas_call(
        place,
        out_shape=[
            S((2, NY * KP), BF), S((2, NY * KP), BF), S((R, 112), F32), S((R, H), F32),
            S((R, 112), F32), S((R, H), F32), S((R, H), F32), S((R, 112), F32),
        ],
        in_specs=[vm] * 3,
        out_specs=[vm] * 8,
        scratch_shapes=[V((2, NY * KP), F32)],
        name="place_outputs",
    )(rows, fd, dla)
    return lo, gt, dget.T, dgl, duet.T, dul, ddet.T, ddl


def solution(mesh):
    return jax.shard_map(
        on_device,
        mesh=mesh,
        in_specs=(
            P(("fsdp", "dp"), None),
            P(("fsdp", "dp"), None),
            P("dp", "fsdp"),
            P("dp", "fsdp"),
            P("dp", "fsdp"),
            P("dp", "fsdp"),
            P("fsdp", "dp"),
            P("fsdp", "dp"),
            P(),
            P(None, "fsdp"),
            P(),
            P(None, "fsdp"),
            P("fsdp", None),
            P(),
        ),
        out_specs=(
            P(("fsdp", "dp"), None),
            P(("fsdp", "dp"), None),
            P("fsdp", None),
            P(None, "fsdp"),
            P("fsdp", None),
            P(None, "fsdp"),
            P("fsdp", None),
            P(None, "fsdp"),
        ),
        check_vma=False,
    )
```

```python
import jax
import jax.numpy as jnp
from jax import lax
from jax.experimental import pallas as pl
from jax.experimental.pallas import tpu as pltpu
from jax.sharding import PartitionSpec as P

NX, NZ, NY = 4, 8, 4
KP, KE, EX = 1792, 1920, 128
G, H, R = 16, 256, 64
NB = 384
BF, F32 = jnp.bfloat16, jnp.float32
MESH = pl.DeviceIdType.MESH


def mm(a, b):
    return jnp.dot(a, b, preferred_element_type=F32)


def mm_nt(a, b):
    return lax.dot_general(a, b, (((1,), (1,)), ((), ())), preferred_element_type=F32)


def mm_tn(a, b):
    return lax.dot_general(a, b, (((0,), (0,)), ((), ())), preferred_element_type=F32)


def kernel(
    tok_hbm, gout_hbm, gs_hbm, us_hbm, ds_hbm, gc_hbm, uc_hbm, dc_hbm, gl_hbm, ul_hbm, det_hbm, get_hbm, uet_hbm, dl_hbm,
    rows_out, fd_out, dla_out,
    tokv, goutv, scv, detv, gcv, ucv, dcv, gev, dlv, ldsem, zsem,
    sf, sends, st1, s1r,
    wgu, wd, wsr,
    aa, agr,
    ext, extp, exr,
    part, rgu, gur,
    parth, rh, hr,
    hb, hall, hallr,
    gb, gall,
    po, pq, rss, rsr, rsrs,
    msg, rows0, rows1, rowss, rowsf, outsem, gota, gotb,
    sp, sa, sar, sb, sc8, sc8r, sd, se, ser, smm, smr,
    res, mb, fd, t3r,
    dlp, dlr, lar,
    gsem,
):
    f = lax.axis_index("fsdp")
    y = lax.axis_index("dp")
    x = lax.div(f, 16)
    z = lax.rem(lax.div(f, 2), 8)
    c = lax.rem(f, 2)
    o = 1 - c

    def fid(xx, zz, cc):
        return xx * 16 + zz * 2 + cc

    def m4(v):
        return lax.rem(v, 4)

    def m8(v):
        return lax.rem(v, 8)

    zp = [m8(z + k) for k in range(NZ)]
    xp = [m4(x + k) for k in range(NX)]
    yp = [m4(y + k) for k in range(NY)]

    def rcopy(src, dst, ssem, rsem, ff, yy):
        return pltpu.make_async_remote_copy(
            src_ref=src, dst_ref=dst, send_sem=ssem, recv_sem=rsem,
            device_id={"fsdp": ff, "dp": yy}, device_id_type=MESH,
        )

    def wait(ref, sem):
        pltpu.make_async_copy(ref, ref, sem).wait()

    def send(src, dst, kind, rsem, ff, yy, own=None):
        ssem = gsem.at[kind]
        if own is None:
            rcopy(src, dst, ssem, rsem, ff, yy).start()
            return

        @pl.when(own)
        def _():
            pltpu.make_async_copy(src, dst, rsem).start()

        @pl.when(jnp.logical_not(own))
        def _():
            rcopy(src, dst, ssem, rsem, ff, yy).start()

    def sent(kind, ref):
        wait(ref, gsem.at[kind])

    loads = [
        pltpu.make_async_copy(get_hbm, gev.at[pl.ds(0, R)], ldsem.at[0]),
        pltpu.make_async_copy(uet_hbm, gev.at[pl.ds(R, R)], ldsem.at[1]),
        pltpu.make_async_copy(dl_hbm, dlv.at[pl.ds(0, R)], ldsem.at[2]),
        pltpu.make_async_copy(gc_hbm, gcv, ldsem.at[3]),
        pltpu.make_async_copy(uc_hbm, ucv, ldsem.at[4]),
        pltpu.make_async_copy(dc_hbm, dcv, ldsem.at[5]),
        pltpu.make_async_copy(tok_hbm, tokv, ldsem.at[6]),
        pltpu.make_async_copy(gout_hbm, goutv, ldsem.at[7]),
        pltpu.make_async_copy(gs_hbm, scv.at[0], ldsem.at[8]),
        pltpu.make_async_copy(gl_hbm, wgu.at[c, pl.ds(KP, R)], ldsem.at[9]),
        pltpu.make_async_copy(ul_hbm, wgu.at[2 + c, pl.ds(KP + R, R)], ldsem.at[10]),
        pltpu.make_async_copy(det_hbm, detv, ldsem.at[11]),
        pltpu.make_async_copy(us_hbm, scv.at[1], ldsem.at[12]),
        pltpu.make_async_copy(ds_hbm, scv.at[2], ldsem.at[13]),
    ]
    for i in (6, 7, 0, 1, 2, 8, 12, 13, 9, 3, 10, 4, 11, 5):
        loads[i].start()

    barrier = pltpu.get_barrier_semaphore()
    peers = []
    for dx in range(NX):
        for dy in range(NY):
            for dc in range(2):
                if dx or dy or dc:
                    peers.append((fid(xp[dx], z, lax.rem(c + dc, 2)), yp[dy]))
    for dz in range(1, NZ):
        peers.append((fid(x, zp[dz], c), y))
    for ff, yy in peers:
        pl.semaphore_signal(barrier, inc=1, device_id={"fsdp": ff, "dp": yy}, device_id_type=MESH)

    dlv[R:EX, :] = jnp.zeros((R, NY * KP), BF)
    for kind, ref in enumerate((tokv, goutv)):
        loads[6 + kind].wait()
        v = ref[...].astype(F32)
        v16 = jnp.concatenate([v, jnp.zeros((14, NY * KP), F32)], axis=0).astype(BF)
        for yy in range(NY):
            for t in range(2):
                for j in range(7):
                    sf[kind, yy, t * 8 + j : t * 8 + j + 1, :] = v[
                        t : t + 1, yy * KP + j * 256 : yy * KP + (j + 1) * 256
                    ]
        if kind == 0:
            loads[0].wait()
            loads[1].wait()
            e = mm_nt(v16, gev[...])
        else:
            loads[2].wait()
            e = mm_nt(v16, dlv[...])
        for yy in range(NY):
            for t in range(2):
                sf[kind, yy, t * 8 + 7 : t * 8 + 8, :] = jnp.concatenate(
                    [e[t : t + 1], jnp.zeros((1, EX), F32)], axis=1
                )
    sends[...] = sf[...].astype(BF)
    pl.semaphore_wait(barrier, len(peers))

    for dz in range(1, NZ):
        pl.semaphore_signal(
            zsem, inc=1, device_id={"fsdp": fid(x, zp[dz], c), "dp": y}, device_id_type=MESH
        )

    src1 = y * 2 + c
    for dy in (2, 1, 3, 0):
        send(
            sends.at[1, yp[dy]], st1.at[x, src1], 0, s1r.at[x], fid(x, z, 1), yp[dy],
            own=(c == 1) if dy == 0 else None,
        )
    for dx in (0, 1, 3, 2):
        for dy in (2, 1, 3, 0):
            send(
                sends.at[0, yp[dy]], st1.at[x, src1], 0, s1r.at[x], fid(xp[dx], z, 0), yp[dy],
                own=(c == 0) if dx == 0 and dy == 0 else None,
            )

    def scale(k, i):
        lane = lax.broadcasted_iota(jnp.int32, (2, 14), 1)
        return jnp.sum(jnp.where(lane == i, scv[k].astype(F32), 0.0), axis=1, keepdims=True)

    def dequant_cols(codes, slot, k):
        def body(i, carry):
            rows = pl.ds(pl.multiple_of(i * 128, 128), 128)
            v = scale(k, i)
            wgu[slot, rows, 0:128] = (codes[rows, 0:128].astype(F32) * v[0:1]).astype(BF)
            wgu[slot, rows, 128:256] = (codes[rows, 128:256].astype(F32) * v[1:2]).astype(BF)
            return carry

        lax.fori_loop(0, 14, body, 0)

    sib = fid(x, z, o)
    for i in (8, 12, 13):
        loads[i].wait()
    loads[3].wait()
    dequant_cols(gcv, c, 0)
    loads[9].wait()
    wgu[c, KP + R :, :] = jnp.zeros((R, H), BF)
    send(wgu.at[c], wgu.at[c], 1, wsr.at[0], sib, y)
    loads[4].wait()
    dequant_cols(ucv, 2 + c, 1)
    wgu[2 + c, KP : KP + R, :] = jnp.zeros((R, H), BF)
    loads[10].wait()
    send(wgu.at[2 + c], wgu.at[2 + c], 2, wsr.at[1], sib, y)
    loads[5].wait()
    loads[11].wait()

    def dequant_down(i, carry):
        cols = pl.ds(pl.multiple_of(i * 128, 128), 128)
        v = scale(2, i)
        wd[c, 0:128, cols] = (dcv[0:128, cols].astype(F32) * v[0:1]).astype(BF)
        wd[c, 128:256, cols] = (dcv[128:256, cols].astype(F32) * v[1:2]).astype(BF)
        return carry

    lax.fori_loop(0, 14, dequant_down, 0)
    det = jnp.concatenate([detv[...].astype(F32), jnp.zeros((R, H), F32)], axis=0)
    wd[c, :, KP:KE] = det.T.astype(BF)
    send(wd.at[c], wd.at[c], 3, wsr.at[2], sib, y)

    def unpack(xx):
        wait(st1.at[xx], s1r.at[xx])
        got = st1[xx].reshape(128, H).astype(F32)
        for h, part_ref in enumerate((gota, gotb)):
            part_ref[...] = got[:, h * 128 : (h + 1) * 128]
            for j in range(8 - h):
                k = 2 * j + h
                aa[z, xx, :, k * 128 : (k + 1) * 128] = part_ref[pl.ds(j, G, stride=8), :].astype(BF)

    flag = jnp.where(y == 0, 1.0, 0.0).astype(F32)

    def masked(v):
        return (v.astype(F32) * flag).astype(BF)

    def have(zz, xx):
        wait(aa.at[zz, xx], agr.at[zz * 4 + xx])

    def fwd(zz, xx, tz, tx):
        send(aa.at[zz, xx], aa.at[zz, xx], 4, agr.at[zz * 4 + xx], fid(tx, tz, c), y)

    zr, zl, zf = zp[1], zp[7], zp[4]
    xrt, xlt, xf = xp[1], xp[3], xp[2]

    def weights():
        wait(wgu.at[o], wsr.at[0])
        wait(wgu.at[2 + o], wsr.at[1])
        wait(wd.at[o], wsr.at[2])

    def front0(zs):
        def body(b, carry):
            a = jnp.concatenate([aa[zz].reshape(64, KE) for zz in zs], axis=0)
            acc = mm(a[:, :KP], wgu[b, 0:KP, :]) + mm(masked(a[:, KP:]), wgu[b, KP:KE, :])
            acc = acc.astype(BF)
            for i, zz in enumerate(zs):
                part[zz, :, b] = acc[i * 64 : (i + 1) * 64].reshape(4, G, H)
            return carry

        lax.fori_loop(0, 4, body, 0)
        for zz in zs:
            for xx in range(NX):
                send(
                    part.at[zz, xx], rgu.at[y, m4(zz)], 6, gur.at[m4(zz)],
                    fid(x, z, lax.div(zz, 4)), m4(zz + xx),
                    own=jnp.logical_and(m4(zz + xx) == y, zz < 4),
                )

    def front1(xx):
        def body(b, carry):
            a = aa[:, xx].reshape(128, KE)
            acc = mm_nt(a[:, :KP], wd[b, :, 0:KP]) + mm_nt(masked(a[:, KP:]), wd[b, :, KP:KE])
            parth[xx, :, b] = acc.astype(BF).reshape(8, G, H)
            return carry

        lax.fori_loop(0, 2, body, 0)
        for zz in range(NZ):
            send(
                parth.at[xx, zz], rh.at[y, zz % 4], 6, hr.at[zz % 4],
                fid(x, z, zz // 4), m4(xx + zz), own=(m4(xx + zz) == y) if zz >= 4 else None,
            )

    def gather0():
        for xx in (x, xrt, xlt, xf):
            unpack(xx)
            fwd(z, xx, zr, x)
            fwd(z, xx, zl, x)
        weights()
        front0([z])
        for k in range(1, 4):
            za, zb = zp[8 - k], zp[k]
            for i, xx in enumerate((x, xrt, xlt, xf)):
                have(za, xx)
                if k < 3 or i < 1:
                    fwd(za, xx, zr, x)
                have(zb, xx)
                if k < 3 or i >= 1:
                    fwd(zb, xx, zl, x)
            front0([za, zb])
        for xx in range(NX):
            have(zf, xx)
        send(aa.at[:, :, :, pl.ds(KP, EX)], ext, 5, exr, sib, y)
        front0([zf])

    def gather1():
        unpack(x)
        for dz in (1, 7, 2, 6):
            fwd(z, x, zp[dz], x)

        def spread(zz, far=False):
            fwd(zz, x, z, xrt)
            fwd(zz, x, z, xlt)
            if far:
                fwd(zz, x, z, xf)

        def xstep(dz, up=False):
            a, b = (xlt, xrt) if up else (xrt, xlt)
            have(zp[dz], a)
            fwd(zp[dz], a, z, b)

        spread(z)
        have(zp[7], x)
        spread(zp[7])
        have(zp[1], x)
        spread(zp[1])
        have(zp[6], x)
        fwd(zp[6], x, zr, x)
        fwd(zp[6], x, zp[2], x)
        have(zp[2], x)
        fwd(zp[2], x, zl, x)
        spread(zp[6])
        spread(zp[2])
        xstep(0, True)
        xstep(7)
        xstep(1, True)
        have(zp[4], x)
        spread(zp[4], True)
        for dz in (5, 3):
            have(zp[dz], x)
            spread(zp[dz])
        xstep(6)
        xstep(2)
        weights()
        front1(x)
        xstep(5, True)
        xstep(3)
        for dz in (0, 1, 4, 5):
            have(zp[dz], xrt)
        front1(xrt)
        for dz in (7, 6, 2, 3, 4):
            have(zp[dz], xlt)
        front1(xlt)
        for dz in range(NZ):
            have(zp[dz], xf)
        send(aa.at[:, :, :, pl.ds(KP, EX)], ext, 5, exr, sib, y)
        front1(xf)

    pl.when(c == 0)(gather0)
    pl.when(c == 1)(gather1)

    def middle(q, carry):
        wait(rgu.at[:, q], gur.at[q])
        wait(rh.at[:, q], hr.at[q])
        for b in range(2):
            g = rgu[0, q, b].astype(F32)
            u = rgu[0, q, 2 + b].astype(F32)
            h = rh[0, q, b].astype(F32)
            for s in range(1, NY):
                g += rgu[s, q, b].astype(F32)
                u += rgu[s, q, 2 + b].astype(F32)
                h += rh[s, q, b].astype(F32)
            sig = jax.nn.sigmoid(g)
            act = g * sig
            hb[q, b] = (act * u).astype(BF)
            gb[q, b] = (h * u * sig * (1.0 + g * (1.0 - sig))).astype(BF)
            gb[q, 2 + b] = (h * act).astype(BF)
        return carry

    lax.fori_loop(0, 4, middle, 0)
    blk = c * 4 + y
    def give_hidden(i):
        qh = m4(z + (0, 3, 1, 2)[i])
        for dy in (2, 1, 3, 0):
            send(hb.at[qh], hall.at[blk, qh], 8, hallr.at[c * 4 + qh], fid(x, z, 0), yp[dy],
                 own=(c == 0) if dy == 0 else None)

    def give_grads(i):
        qg = m4(y + 8 - x - (2, 1, 3, 0)[i])
        for dy in (2, 1, 3, 0):
            send(gb.at[qg], gall.at[blk, qg], 7, hallr.at[m4(y + 4 - qg)], fid(x, z, 1), yp[dy],
                 own=(c == 1) if dy == 0 else None)

    for fn, i in (
        (give_hidden, 0), (give_hidden, 1), (give_hidden, 2), (give_grads, 0), (give_grads, 1), (give_grads, 2), (give_hidden, 3), (give_grads, 3),
    ):
        fn(i)

    def small_a():
        mids = jnp.zeros((64, EX), F32)
        backs = jnp.zeros((64, EX), F32)
        for b in range(2):
            mids += mm(hb[:, b].reshape(64, H), wd[b, :, KP:KE])
        for b in range(4):
            backs += mm_nt(gb[:, b].reshape(64, H), wgu[b, KP:KE, :])
        sp[:, :, 0:EX] = mids.astype(BF).reshape(4, G, EX)
        sp[:, :, EX : 2 * EX] = backs.astype(BF).reshape(4, G, EX)
        for q in range(NX):
            send(sp.at[q], sa.at[x], 9, sar, fid(q, z, c), y, own=x == q)

    small_a()

    def small_b():
        wait(sa, sar)
        v = sa[0].astype(F32)
        for i in range(1, NX):
            v += sa[i].astype(F32)
        sb[...] = v.astype(BF)
        for dz in (4, 3, 5, 2, 6, 1, 7):
            send(sb, sc8.at[z], 10, sc8r, fid(x, zp[dz], c), y)

    def small_c():
        v = sb[...].astype(F32)
        wait(sc8.at[pl.ds(0, NZ - 1)], sc8r)
        for dz in range(1, NZ):
            v += sc8[zp[dz]].astype(F32)
        sd[...] = v.astype(BF)
        for dx in (2, 1, 3):
            send(sd, se.at[x], 11, ser, fid(xp[dx], z, c), y)

    def small_d():
        wait(se.at[pl.ds(0, NX - 1)], ser)
        se[x] = sd[...]
        for cc in range(2):
            lanes = pl.ds((1 - cc) * EX, EX)
            send(se.at[:, :, lanes], smm.at[blk], 12 + cc, smr, fid(x, z, cc), x,
                 own=jnp.logical_and(c == cc, y == x))

    def small_e():
        wait(smm, smr)
        small = jnp.concatenate(
            [smm[(zz // 4) * 4 + (xx + zz) % 4, zz % 4] for zz in range(NZ) for xx in range(NX)], axis=0
        )
        first = lax.div(z * 224, 128) * 128
        lead = z * 224 - first
        win = pl.ds(pl.multiple_of(first, 128), 384)
        res[...] = mm_tn(aa[:, :, :, win].reshape(512, 384), small)
        for cc in range(2):
            mb[cc, 0:112, :] = res[pl.ds(pl.multiple_of(lead + cc * 112, 8), 112), :].astype(BF)
        for dy in (2, 1, 3, 0):
            for cc in range(2):
                send(
                    mb.at[cc], fd.at[c], 17, t3r.at[c], fid(x, z, cc), yp[dy],
                    own=(c == cc) if dy == 0 else None,
                )

    def order_ext():
        wait(ext, exr)
        for i in range(8):
            for q in range(4):
                zz = (i // 4) * 4 + q
                extp[(i * 4 + q) * G : (i * 4 + q + 1) * G, :] = ext[zz, (i % 4 + 8 - zz) % 4]

    def ring(d, slot, v, tgt):
        k = d * 16 + slot
        rss[k] = v.astype(BF)
        send(rss.at[k], rsr.at[k], 14, rsrs.at[k], tgt, y)

    def come(d, slot):
        k = d * 16 + slot
        wait(rsr.at[k], rsrs.at[k])
        return rsr[k].astype(F32)

    mycols = pl.ds(pl.multiple_of(y * KP, 128), KP)

    def last(g, v, back, xx, zz, here, rows, rsem, slot):
        v = v[:, :KP] + mm(v[:, KP:KE].astype(BF), back[:, mycols])
        for j in range(7):
            gota[pl.ds(j, G, stride=8), :] = v[:, j * 256 : j * 256 + 128]
            gotb[pl.ds(j, G, stride=8), :] = v[:, j * 256 + 128 : (j + 1) * 256]
        msg[g * 8 : (g + 1) * 8, :, 0:128] = gota[...].astype(BF).reshape(8, G, 128)
        msg[g * 8 : (g + 1) * 8, :, 128:256] = gotb[...].astype(BF).reshape(8, G, 128)
        for dy in (2, 1, 3, 0):
            for cc in range(2):
                send(
                    msg.at[g * 8 + yp[dy] * 2 + cc], rows.at[slot, y], 16, rsem, fid(xx, zz, cc), yp[dy],
                    own=jnp.logical_and(c == cc, here) if dy == 0 else None,
                )

    def out0(ts):
        for t in ts:
            wait(hall.at[pl.ds(lax.div(t, 4) * 4, 4), m4(t)], hallr.at[t])

        def rows(kb):
            return jnp.concatenate(
                [hall[lax.div(t, 4) * 4 + m4(t + xx), m4(t), kb] for t in ts for xx in range(NX)], axis=0
            )

        def body(nb, carry):
            cols = pl.ds(pl.multiple_of(nb * NB, 128), NB)
            po[0 : 64 * len(ts), cols] = mm(rows(0), wd[0, :, cols]) + mm(rows(1), wd[1, :, cols])
            return carry

        lax.fori_loop(0, KE // NB, body, 0)

    def scatter0():
        right, left = fid(x, zr, 0), fid(x, zl, 0)
        out0([zf])
        for xx in range(2):
            ring(0, xx, po[xx * G : (xx + 1) * G, :], fid(x, zp[2], 0))
            ring(1, xx + 2, po[(xx + 2) * G : (xx + 3) * G, :], fid(x, zp[6], 0))
        for s in range(1, 4):
            out0([zp[4 - s], zp[4 + s]])
            for xx in range(NX):
                for d, tgt in ((0, right), (1, left)):
                    v = po[(4 * d + xx) * G : (4 * d + xx + 1) * G, :]
                    if s > 1:
                        v = v + come(d, (s - 1) * 4 + xx)
                    if s == 2 and xx // 2 == d:
                        v = v + come(d, xx)
                    ring(d, s * 4 + xx, v, tgt)
            (small_b, small_c, small_d)[s - 1]()
        out0([z])
        pl.semaphore_wait(zsem, NZ - 1)
        order_ext()
        for b in range(2):
            dlp[b] = mm_tn(extp[...], hall[:, :, b].reshape(512, H))[0:R]
        send(dlp.at[1], dlr.at[0], 15, lar.at[0], sib, y)
        for xx in range(NX):
            v = po[xx * G : (xx + 1) * G, :] + come(0, 12 + xx) + come(1, 12 + xx)
            last(xx, v, dlv, xx, z, x == xx, rows0, rowss.at[0], x)
        pl.when(x == y)(small_e)
        sent(4, rsr.at[pl.ds(0, 28)])
        sent(6, part.at[pl.ds(0, 7)])
        sent(7, part.at[pl.ds(0, 4)])
        sent(8, part.at[pl.ds(0, 3), pl.ds(0, 2)])
        sent(14, rsr.at[pl.ds(0, 28)])
        sent(15, dlp.at[0])
        sent(16, msg.at[pl.ds(0, 31)])
        pl.when(x == y)(lambda: sent(17, part.at[pl.ds(0, 7), 0]))

    def out1(t, dst):
        wait(gall.at[:, 0], hallr.at[t])

        def rows(b):
            return jnp.concatenate(
                [gall[(zz // 4) * 4 + m4(t + zz), zz % 4, b] for zz in range(NZ)], axis=0
            )

        def body(nb, carry):
            cols = pl.ds(pl.multiple_of(nb * NB, 128), NB)
            acc = mm_nt(rows(0), wgu[0, cols, :])
            for b in range(1, 4):
                acc += mm_nt(rows(b), wgu[b, cols, :])
            dst[:, cols] = acc
            return carry

        lax.fori_loop(0, KE // NB, body, 0)

    def scatter1():
        right, left = fid(xrt, z, 1), fid(xlt, z, 1)
        out1(xf, po)
        for zz in range(4):
            ring(0, zz, po[zz * G : (zz + 1) * G, :], right)
            ring(1, zz + 4, po[(zz + 4) * G : (zz + 5) * G, :], left)
        out1(xrt, po)
        for zz in range(4, 8):
            ring(0, 8 + zz, po[zz * G : (zz + 1) * G, :], right)
        out1(xlt, pq)
        for zz in range(4):
            ring(1, 8 + zz, pq[zz * G : (zz + 1) * G, :], left)
        for zz in range(4):
            ring(0, 8 + zz, po[zz * G : (zz + 1) * G, :] + come(0, zz), right)
            ring(1, 12 + zz, pq[(zz + 4) * G : (zz + 5) * G, :] + come(1, zz + 4), left)
        small_b()
        out1(x, po)
        pl.semaphore_wait(zsem, NZ - 1)
        small_c()
        for i, zz in enumerate((0, 4, 1, 5, 2, 6, 3, 7)):
            v = po[zz * G : (zz + 1) * G, :] + come(0, 8 + zz) + come(1, 8 + zz)
            last(zz, v, gev, x, zz, z == zz, rows1, rowss.at[1], z)
            if i == 3:
                small_d()
        order_ext()
        for b in range(4):
            grad = mm_tn(extp[...], gall[:, :, b].reshape(512, H))
            dlp[b] = grad[0:R] if b < 2 else grad[R:EX]
        send(dlp.at[0], dlr.at[0], 15, lar.at[0], sib, y)
        send(dlp.at[2], dlr.at[1], 15, lar.at[1], sib, y)
        pl.when(x == y)(small_e)
        sent(4, rsr.at[pl.ds(0, 31)])
        sent(6, part.at[pl.ds(0, 7), pl.ds(0, 2)])
        sent(7, part.at[pl.ds(0, 3)])
        sent(8, part.at[pl.ds(0, 2)])
        sent(14, rsr.at[pl.ds(0, 24)])
        sent(15, dlp.at[pl.ds(0, 2)])
        sent(16, msg.at[pl.ds(0, 63)])
        pl.when(x == y)(lambda: sent(17, part.at[pl.ds(0, 7), 0]))

    pl.when(c == 0)(scatter0)
    pl.when(c == 1)(scatter1)

    def give(pairs):
        for i, (ref, sem) in enumerate(pairs):
            if sem is not None:
                wait(ref, sem)
            pltpu.make_async_copy(ref, dla_out.at[i], outsem.at[i]).start()

    pl.when(c == 0)(lambda: give(((dlp.at[0], None), (dlr.at[0], lar.at[0]), (dlr.at[1], lar.at[1]))))
    pl.when(c == 1)(lambda: give(((dlr.at[0], lar.at[0]), (dlp.at[1], None), (dlp.at[3], None))))
    wait(fd.at[0], t3r.at[0])
    wait(fd.at[1], t3r.at[1])
    out_fd = pltpu.make_async_copy(fd, fd_out, outsem.at[3])
    out_fd.start()
    for kind, (rows, n) in enumerate(((rows0, NX), (rows1, NZ))):
        wait(rows, rowss.at[kind])
        v = rows[0].astype(F32)
        for i in range(1, n):
            v += rows[i].astype(F32)
        rowsf[kind] = v
    out_rows = pltpu.make_async_copy(rowsf, rows_out, outsem.at[4])
    out_rows.start()
    for i in range(3):
        wait(dlp.at[0], outsem.at[i])
    out_fd.wait()
    out_rows.wait()
    sent(0, msg.at[pl.ds(0, 19)])
    sent(1, wgu.at[0])
    sent(2, wgu.at[0])
    sent(3, wd.at[0])
    sent(5, ext)
    sent(9, msg.at[pl.ds(0, 3)])
    sent(10, msg.at[pl.ds(0, 7)])
    sent(11, msg.at[pl.ds(0, 3)])
    for cc in range(2):
        @pl.when(jnp.logical_not(jnp.logical_and(c == cc, y == x)))
        def _(cc=cc):
            sent(12 + cc, smm.at[0])


def place(rows_ref, fd_ref, dla_ref, lo, gt, dget, dgl, duet, dul, ddet, ddl, row):
    for kind, ref in enumerate((lo, gt)):
        for yy in range(NY):
            for t in range(2):
                for j in range(7):
                    row[t : t + 1, yy * KP + j * 256 : yy * KP + (j + 1) * 256] = rows_ref[
                        kind, yy, t * 8 + j : t * 8 + j + 1, :
                    ]
        ref[...] = row[...].astype(BF)
    v = fd_ref[0].astype(F32).T
    dget[...] = v[:R, :112]
    duet[...] = v[R:EX, :112]
    ddl[...] = fd_ref[1].astype(F32).T[:R, :112]
    ddet[...] = dla_ref[0]
    dgl[...] = dla_ref[1]
    dul[...] = dla_ref[2]


def dma(*shape):
    return pltpu.SemaphoreType.DMA(shape)


def on_device(
    tokens, grad_out, gate_codes, gate_scales, up_codes, up_scales, down_codes, down_scales,
    gate_enter, gate_leave, up_enter, up_leave, down_enter, down_leave,
):
    vm = pl.BlockSpec(memory_space=pltpu.VMEM)
    hb = pl.BlockSpec(memory_space=pltpu.HBM)
    V = pltpu.VMEM
    one = pltpu.SemaphoreType.DMA
    scratch = [
        V((2, NY * KP), BF), V((2, NY * KP), BF), V((3, 2, 14), BF), V((R, H), BF),
        V((KP, H), BF), V((KP, H), BF), V((H, KP), BF), V((EX, NY * KP), BF), V((EX, NY * KP), BF), dma(14),
        pltpu.SemaphoreType.REGULAR,
        V((2, NY, G, H), F32), V((2, NY, G, H), BF), V((NX, 8, G, H), BF), dma(NX),
        V((4, KE, H), BF), V((2, H, KE), BF), dma(3),
        V((NZ, NX, G, KE), BF), dma(32),
        V((NZ, NX, G, EX), BF), V((512, EX), BF), one,
        V((NZ, NX, 4, G, H), BF), V((NY, 4, 4, G, H), BF), dma(4),
        V((NX, NZ, 2, G, H), BF), V((NY, 4, 2, G, H), BF), dma(4),
        V((4, 2, G, H), BF), V((8, 4, 2, G, H), BF), dma(8),
        V((4, 4, G, H), BF), V((8, 4, 4, G, H), BF),
        V((128, KE), F32), V((128, KE), F32), V((32, G, KE), BF), V((32, G, KE), BF), dma(32),
        V((64, G, H), BF), V((NX, NY, G, H), BF), V((NZ, NY, G, H), BF), dma(2),
        V((2, NY, G, H), F32), dma(5), V((128, 128), F32), V((128, 128), F32),
        V((4, G, H), BF), V((NX, G, H), BF), one, V((G, H), BF), V((NZ, G, H), BF), one,
        V((G, H), BF), V((NX, G, H), BF), one, V((8, 4, G, EX), BF), one,
        V((384, EX), F32), V((2, EX, EX), BF), V((2, EX, EX), BF), dma(2),
        V((4, R, H), F32), V((2, R, H), F32), dma(2),
        dma(18),
    ]
    S = jax.ShapeDtypeStruct
    rows, fd, dla = pl.pallas_call(
        kernel,
        out_shape=[S((2, NY, G, H), F32), S((2, EX, EX), BF), S((3, R, H), F32)],
        in_specs=[hb] * 14,
        out_specs=[hb] * 3,
        scratch_shapes=scratch,
        compiler_params=pltpu.CompilerParams(
            collective_id=0, has_side_effects=True, vmem_limit_bytes=63 * 1024 * 1024
        ),
        name="lora_ffn_step",
    )(
        tokens, grad_out, gate_scales.T, up_scales.T, down_scales, gate_codes, up_codes, down_codes, gate_leave, up_leave, down_enter.T,
        gate_enter.T, up_enter.T, down_leave,
    )
    lo, gt, dget, dgl, duet, dul, ddet, ddl = pl.pallas_call(
        place,
        out_shape=[
            S((2, NY * KP), BF), S((2, NY * KP), BF), S((R, 112), F32), S((R, H), F32),
            S((R, 112), F32), S((R, H), F32), S((R, H), F32), S((R, 112), F32),
        ],
        in_specs=[vm] * 3,
        out_specs=[vm] * 8,
        scratch_shapes=[V((2, NY * KP), F32)],
        name="place_outputs",
    )(rows, fd, dla)
    return lo, gt, dget.T, dgl, duet.T, dul, ddet.T, ddl


def solution(mesh):
    return jax.shard_map(
        on_device,
        mesh=mesh,
        in_specs=(
            P(("fsdp", "dp"), None),
            P(("fsdp", "dp"), None),
            P("dp", "fsdp"),
            P("dp", "fsdp"),
            P("dp", "fsdp"),
            P("dp", "fsdp"),
            P("fsdp", "dp"),
            P("fsdp", "dp"),
            P(),
            P(None, "fsdp"),
            P(),
            P(None, "fsdp"),
            P("fsdp", None),
            P(),
        ),
        out_specs=(
            P(("fsdp", "dp"), None),
            P(("fsdp", "dp"), None),
            P("fsdp", None),
            P(None, "fsdp"),
            P("fsdp", None),
            P(None, "fsdp"),
            P("fsdp", None),
            P(None, "fsdp"),
        ),
        check_vma=False,
    )
```

```python
import jax
import jax.numpy as jnp
from jax import lax
from jax.experimental import pallas as pl
from jax.experimental.pallas import tpu as pltpu
from jax.sharding import PartitionSpec as P

NX, NZ, NY = 4, 8, 4
KP, KE, EX = 1792, 1920, 128
G, H, R = 16, 256, 64
NB = 384
BF, F32 = jnp.bfloat16, jnp.float32
MESH = pl.DeviceIdType.MESH


def mm(a, b):
    return jnp.dot(a, b, preferred_element_type=F32)


def mm_nt(a, b):
    return lax.dot_general(a, b, (((1,), (1,)), ((), ())), preferred_element_type=F32)


def mm_tn(a, b):
    return lax.dot_general(a, b, (((0,), (0,)), ((), ())), preferred_element_type=F32)


def kernel(
    tok_hbm, gout_hbm, gs_hbm, us_hbm, ds_hbm, gc_hbm, uc_hbm, dc_hbm, gl_hbm, ul_hbm, det_hbm, get_hbm, uet_hbm, dl_hbm,
    rows_out, fd_out, dla_out,
    tokv, goutv, scv, detv, gcv, ucv, dcv, gev, dlv, ldsem, zsem,
    sf, sends, st1, s1r,
    wgu, wd, wsr,
    aa, agr,
    ext, extp, exr,
    part, rgu, gur,
    parth, rh, hr,
    hb, hall, hallr,
    gb, gall,
    po, pq, rss, rsr, rsrs,
    msg, rows0, rows1, rowss, rowsf, outsem, gota, gotb,
    sp, sa, sar, sb, sc8, sc8r, sd, se, ser, smm, smr,
    res, mb, fd, t3r,
    dlp, dlr, lar,
    gsem,
):
    f = lax.axis_index("fsdp")
    y = lax.axis_index("dp")
    x = lax.div(f, 16)
    z = lax.rem(lax.div(f, 2), 8)
    c = lax.rem(f, 2)
    o = 1 - c

    def fid(xx, zz, cc):
        return xx * 16 + zz * 2 + cc

    def m4(v):
        return lax.rem(v, 4)

    def m8(v):
        return lax.rem(v, 8)

    zp = [m8(z + k) for k in range(NZ)]
    xp = [m4(x + k) for k in range(NX)]
    yp = [m4(y + k) for k in range(NY)]

    def rcopy(src, dst, ssem, rsem, ff, yy):
        return pltpu.make_async_remote_copy(
            src_ref=src, dst_ref=dst, send_sem=ssem, recv_sem=rsem,
            device_id={"fsdp": ff, "dp": yy}, device_id_type=MESH,
        )

    def wait(ref, sem):
        pltpu.make_async_copy(ref, ref, sem).wait()

    def send(src, dst, kind, rsem, ff, yy, own=None):
        ssem = gsem.at[kind]
        if own is None:
            rcopy(src, dst, ssem, rsem, ff, yy).start()
            return

        @pl.when(own)
        def _():
            pltpu.make_async_copy(src, dst, rsem).start()

        @pl.when(jnp.logical_not(own))
        def _():
            rcopy(src, dst, ssem, rsem, ff, yy).start()

    def sent(kind, ref):
        wait(ref, gsem.at[kind])

    loads = [
        pltpu.make_async_copy(get_hbm, gev.at[pl.ds(0, R)], ldsem.at[0]),
        pltpu.make_async_copy(uet_hbm, gev.at[pl.ds(R, R)], ldsem.at[1]),
        pltpu.make_async_copy(dl_hbm, dlv.at[pl.ds(0, R)], ldsem.at[2]),
        pltpu.make_async_copy(gc_hbm, gcv, ldsem.at[3]),
        pltpu.make_async_copy(uc_hbm, ucv, ldsem.at[4]),
        pltpu.make_async_copy(dc_hbm, dcv, ldsem.at[5]),
        pltpu.make_async_copy(tok_hbm, tokv, ldsem.at[6]),
        pltpu.make_async_copy(gout_hbm, goutv, ldsem.at[7]),
        pltpu.make_async_copy(gs_hbm, scv.at[0], ldsem.at[8]),
        pltpu.make_async_copy(gl_hbm, wgu.at[c, pl.ds(KP, R)], ldsem.at[9]),
        pltpu.make_async_copy(ul_hbm, wgu.at[2 + c, pl.ds(KP + R, R)], ldsem.at[10]),
        pltpu.make_async_copy(det_hbm, detv, ldsem.at[11]),
        pltpu.make_async_copy(us_hbm, scv.at[1], ldsem.at[12]),
        pltpu.make_async_copy(ds_hbm, scv.at[2], ldsem.at[13]),
    ]
    for i in (6, 7, 0, 1, 2, 8, 12, 13, 9, 3, 10, 4, 11, 5):
        loads[i].start()

    barrier = pltpu.get_barrier_semaphore()
    peers = []
    for dx in range(NX):
        for dy in range(NY):
            for dc in range(2):
                if dx or dy or dc:
                    peers.append((fid(xp[dx], z, lax.rem(c + dc, 2)), yp[dy]))
    for dz in range(1, NZ):
        peers.append((fid(x, zp[dz], c), y))
    for ff, yy in peers:
        pl.semaphore_signal(barrier, inc=1, device_id={"fsdp": ff, "dp": yy}, device_id_type=MESH)

    dlv[R:EX, :] = jnp.zeros((R, NY * KP), BF)
    for kind, ref in enumerate((tokv, goutv)):
        loads[6 + kind].wait()
        v = ref[...].astype(F32)
        v16 = jnp.concatenate([v, jnp.zeros((14, NY * KP), F32)], axis=0).astype(BF)
        for yy in range(NY):
            for t in range(2):
                for j in range(7):
                    sf[kind, yy, t * 8 + j : t * 8 + j + 1, :] = v[
                        t : t + 1, yy * KP + j * 256 : yy * KP + (j + 1) * 256
                    ]
        if kind == 0:
            loads[0].wait()
            loads[1].wait()
            e = mm_nt(v16, gev[...])
        else:
            loads[2].wait()
            e = mm_nt(v16, dlv[...])
        for yy in range(NY):
            for t in range(2):
                sf[kind, yy, t * 8 + 7 : t * 8 + 8, :] = jnp.concatenate(
                    [e[t : t + 1], jnp.zeros((1, EX), F32)], axis=1
                )
    sends[...] = sf[...].astype(BF)
    pl.semaphore_wait(barrier, len(peers))

    for dz in range(1, NZ):
        pl.semaphore_signal(
            zsem, inc=1, device_id={"fsdp": fid(x, zp[dz], c), "dp": y}, device_id_type=MESH
        )

    src1 = y * 2 + c
    for dy in (2, 1, 3, 0):
        send(
            sends.at[1, yp[dy]], st1.at[x, src1], 0, s1r.at[x], fid(x, z, 1), yp[dy],
            own=(c == 1) if dy == 0 else None,
        )
    for dx in (0, 1, 3, 2):
        for dy in (2, 1, 3, 0):
            send(
                sends.at[0, yp[dy]], st1.at[x, src1], 0, s1r.at[x], fid(xp[dx], z, 0), yp[dy],
                own=(c == 0) if dx == 0 and dy == 0 else None,
            )

    def scale(k, i):
        lane = lax.broadcasted_iota(jnp.int32, (2, 14), 1)
        return jnp.sum(jnp.where(lane == i, scv[k].astype(F32), 0.0), axis=1, keepdims=True)

    def dequant_cols(codes, slot, k):
        def body(i, carry):
            rows = pl.ds(pl.multiple_of(i * 128, 128), 128)
            v = scale(k, i)
            wgu[slot, rows, 0:128] = (codes[rows, 0:128].astype(F32) * v[0:1]).astype(BF)
            wgu[slot, rows, 128:256] = (codes[rows, 128:256].astype(F32) * v[1:2]).astype(BF)
            return carry

        lax.fori_loop(0, 14, body, 0)

    sib = fid(x, z, o)
    for i in (8, 12, 13):
        loads[i].wait()
    loads[3].wait()
    dequant_cols(gcv, c, 0)
    loads[9].wait()
    wgu[c, KP + R :, :] = jnp.zeros((R, H), BF)
    send(wgu.at[c], wgu.at[c], 1, wsr.at[0], sib, y)
    loads[4].wait()
    dequant_cols(ucv, 2 + c, 1)
    wgu[2 + c, KP : KP + R, :] = jnp.zeros((R, H), BF)
    loads[10].wait()
    send(wgu.at[2 + c], wgu.at[2 + c], 2, wsr.at[1], sib, y)
    loads[5].wait()
    loads[11].wait()

    def dequant_down(i, carry):
        cols = pl.ds(pl.multiple_of(i * 128, 128), 128)
        v = scale(2, i)
        wd[c, 0:128, cols] = (dcv[0:128, cols].astype(F32) * v[0:1]).astype(BF)
        wd[c, 128:256, cols] = (dcv[128:256, cols].astype(F32) * v[1:2]).astype(BF)
        return carry

    lax.fori_loop(0, 14, dequant_down, 0)
    det = jnp.concatenate([detv[...].astype(F32), jnp.zeros((R, H), F32)], axis=0)
    wd[c, :, KP:KE] = det.T.astype(BF)
    send(wd.at[c], wd.at[c], 3, wsr.at[2], sib, y)

    def unpack(xx):
        wait(st1.at[xx], s1r.at[xx])
        got = st1[xx].reshape(128, H).astype(F32)
        for h, part_ref in enumerate((gota, gotb)):
            part_ref[...] = got[:, h * 128 : (h + 1) * 128]
            for j in range(8 - h):
                k = 2 * j + h
                aa[z, xx, :, k * 128 : (k + 1) * 128] = part_ref[pl.ds(j, G, stride=8), :].astype(BF)

    flag = jnp.where(y == 0, 1.0, 0.0).astype(F32)

    def masked(v):
        return (v.astype(F32) * flag).astype(BF)

    def have(zz, xx):
        wait(aa.at[zz, xx], agr.at[zz * 4 + xx])

    def fwd(zz, xx, tz, tx):
        send(aa.at[zz, xx], aa.at[zz, xx], 4, agr.at[zz * 4 + xx], fid(tx, tz, c), y)

    zr, zl, zf = zp[1], zp[7], zp[4]
    xrt, xlt, xf = xp[1], xp[3], xp[2]

    def weights():
        wait(wgu.at[o], wsr.at[0])
        wait(wgu.at[2 + o], wsr.at[1])
        wait(wd.at[o], wsr.at[2])

    def front0(zs):
        def body(b, carry):
            a = jnp.concatenate([aa[zz].reshape(64, KE) for zz in zs], axis=0)
            acc = mm(a[:, :KP], wgu[b, 0:KP, :]) + mm(masked(a[:, KP:]), wgu[b, KP:KE, :])
            acc = acc.astype(BF)
            for i, zz in enumerate(zs):
                part[zz, :, b] = acc[i * 64 : (i + 1) * 64].reshape(4, G, H)
            return carry

        lax.fori_loop(0, 4, body, 0)
        for zz in zs:
            for xx in range(NX):
                send(
                    part.at[zz, xx], rgu.at[y, m4(zz)], 6, gur.at[m4(zz)],
                    fid(x, z, lax.div(zz, 4)), m4(zz + xx),
                    own=jnp.logical_and(m4(zz + xx) == y, zz < 4),
                )

    def front1(xx):
        def body(b, carry):
            a = aa[:, xx].reshape(128, KE)
            acc = mm_nt(a[:, :KP], wd[b, :, 0:KP]) + mm_nt(masked(a[:, KP:]), wd[b, :, KP:KE])
            parth[xx, :, b] = acc.astype(BF).reshape(8, G, H)
            return carry

        lax.fori_loop(0, 2, body, 0)
        for zz in range(NZ):
            send(
                parth.at[xx, zz], rh.at[y, zz % 4], 6, hr.at[zz % 4],
                fid(x, z, zz // 4), m4(xx + zz), own=(m4(xx + zz) == y) if zz >= 4 else None,
            )

    def gather0():
        for xx in (x, xrt, xlt, xf):
            unpack(xx)
            fwd(z, xx, zr, x)
            fwd(z, xx, zl, x)
        weights()
        front0([z])
        for k in range(1, 4):
            za, zb = zp[8 - k], zp[k]
            for i, xx in enumerate((x, xrt, xlt, xf)):
                have(za, xx)
                if k < 3:
                    fwd(za, xx, zr, x)
                if k == 2 and i < 2:
                    fwd(za, xx, zp[2], x)
                have(zb, xx)
                if k < 3:
                    fwd(zb, xx, zl, x)
                if k == 2 and i >= 2:
                    fwd(zb, xx, zp[6], x)
            front0([za, zb])
        for xx in range(NX):
            have(zf, xx)
        send(aa.at[:, :, :, pl.ds(KP, EX)], ext, 5, exr, sib, y)
        front0([zf])

    def gather1():
        unpack(x)
        for dz in (1, 7, 2, 6):
            fwd(z, x, zp[dz], x)

        def spread(zz, far=False):
            fwd(zz, x, z, xrt)
            fwd(zz, x, z, xlt)
            if far:
                fwd(zz, x, z, xf)

        def xstep(dz, up=False):
            a, b = (xlt, xrt) if up else (xrt, xlt)
            have(zp[dz], a)
            fwd(zp[dz], a, z, b)

        spread(z)
        have(zp[7], x)
        spread(zp[7])
        have(zp[1], x)
        spread(zp[1])
        have(zp[6], x)
        fwd(zp[6], x, zr, x)
        fwd(zp[6], x, zp[2], x)
        have(zp[2], x)
        fwd(zp[2], x, zl, x)
        spread(zp[6])
        spread(zp[2])
        xstep(0, True)
        xstep(7)
        xstep(1, True)
        have(zp[4], x)
        spread(zp[4], True)
        for dz in (5, 3):
            have(zp[dz], x)
            spread(zp[dz])
        xstep(6)
        xstep(2)
        weights()
        front1(x)
        xstep(5, True)
        xstep(3)
        for dz in (0, 1, 4, 5):
            have(zp[dz], xrt)
        front1(xrt)
        for dz in (7, 6, 2, 3, 4):
            have(zp[dz], xlt)
        front1(xlt)
        for dz in range(NZ):
            have(zp[dz], xf)
        send(aa.at[:, :, :, pl.ds(KP, EX)], ext, 5, exr, sib, y)
        front1(xf)

    pl.when(c == 0)(gather0)
    pl.when(c == 1)(gather1)

    def middle(q, carry):
        wait(rgu.at[:, q], gur.at[q])
        wait(rh.at[:, q], hr.at[q])
        for b in range(2):
            g = rgu[0, q, b].astype(F32)
            u = rgu[0, q, 2 + b].astype(F32)
            h = rh[0, q, b].astype(F32)
            for s in range(1, NY):
                g += rgu[s, q, b].astype(F32)
                u += rgu[s, q, 2 + b].astype(F32)
                h += rh[s, q, b].astype(F32)
            sig = jax.nn.sigmoid(g)
            act = g * sig
            hb[q, b] = (act * u).astype(BF)
            gb[q, b] = (h * u * sig * (1.0 + g * (1.0 - sig))).astype(BF)
            gb[q, 2 + b] = (h * act).astype(BF)
        return carry

    lax.fori_loop(0, 4, middle, 0)
    blk = c * 4 + y
    def give_hidden(i):
        qh = m4(z + (0, 3, 1, 2)[i])
        for dy in (2, 1, 3, 0):
            send(hb.at[qh], hall.at[blk, qh], 8, hallr.at[c * 4 + qh], fid(x, z, 0), yp[dy],
                 own=(c == 0) if dy == 0 else None)

    def give_grads(i):
        qg = m4(y + 8 - x - (2, 1, 3, 0)[i])
        for dy in (2, 1, 3, 0):
            send(gb.at[qg], gall.at[blk, qg], 7, hallr.at[m4(y + 4 - qg)], fid(x, z, 1), yp[dy],
                 own=(c == 1) if dy == 0 else None)

    for fn, i in (
        (give_hidden, 0), (give_hidden, 1), (give_hidden, 2), (give_grads, 0), (give_grads, 1), (give_grads, 2), (give_hidden, 3), (give_grads, 3),
    ):
        fn(i)

    def small_a():
        mids = jnp.zeros((64, EX), F32)
        backs = jnp.zeros((64, EX), F32)
        for b in range(2):
            mids += mm(hb[:, b].reshape(64, H), wd[b, :, KP:KE])
        for b in range(4):
            backs += mm_nt(gb[:, b].reshape(64, H), wgu[b, KP:KE, :])
        sp[:, :, 0:EX] = mids.astype(BF).reshape(4, G, EX)
        sp[:, :, EX : 2 * EX] = backs.astype(BF).reshape(4, G, EX)
        for q in range(NX):
            send(sp.at[q], sa.at[x], 9, sar, fid(q, z, c), y, own=x == q)

    small_a()

    def small_b():
        wait(sa, sar)
        v = sa[0].astype(F32)
        for i in range(1, NX):
            v += sa[i].astype(F32)
        sb[...] = v.astype(BF)
        for dz in (4, 3, 5, 2, 6, 1, 7):
            send(sb, sc8.at[z], 10, sc8r, fid(x, zp[dz], c), y)

    def small_c():
        v = sb[...].astype(F32)
        wait(sc8.at[pl.ds(0, NZ - 1)], sc8r)
        for dz in range(1, NZ):
            v += sc8[zp[dz]].astype(F32)
        sd[...] = v.astype(BF)
        for dx in (2, 1, 3):
            send(sd, se.at[x], 11, ser, fid(xp[dx], z, c), y)

    def small_d():
        wait(se.at[pl.ds(0, NX - 1)], ser)
        se[x] = sd[...]
        for cc in range(2):
            lanes = pl.ds((1 - cc) * EX, EX)
            send(se.at[:, :, lanes], smm.at[blk], 12 + cc, smr, fid(x, z, cc), x,
                 own=jnp.logical_and(c == cc, y == x))

    def small_e():
        wait(smm, smr)
        small = jnp.concatenate(
            [smm[(zz // 4) * 4 + (xx + zz) % 4, zz % 4] for zz in range(NZ) for xx in range(NX)], axis=0
        )
        first = lax.div(z * 224, 128) * 128
        lead = z * 224 - first
        win = pl.ds(pl.multiple_of(first, 128), 384)
        res[...] = mm_tn(aa[:, :, :, win].reshape(512, 384), small)
        for cc in range(2):
            mb[cc, 0:112, :] = res[pl.ds(pl.multiple_of(lead + cc * 112, 8), 112), :].astype(BF)
        for dy in (2, 1, 3, 0):
            for cc in range(2):
                send(
                    mb.at[cc], fd.at[c], 17, t3r.at[c], fid(x, z, cc), yp[dy],
                    own=(c == cc) if dy == 0 else None,
                )

    def order_ext():
        wait(ext, exr)
        for i in range(8):
            for q in range(4):
                zz = (i // 4) * 4 + q
                extp[(i * 4 + q) * G : (i * 4 + q + 1) * G, :] = ext[zz, (i % 4 + 8 - zz) % 4]

    def ring(d, slot, v, tgt):
        k = d * 16 + slot
        rss[k] = v.astype(BF)
        send(rss.at[k], rsr.at[k], 14, rsrs.at[k], tgt, y)

    def come(d, slot):
        k = d * 16 + slot
        wait(rsr.at[k], rsrs.at[k])
        return rsr[k].astype(F32)

    mycols = pl.ds(pl.multiple_of(y * KP, 128), KP)

    def last(g, v, back, xx, zz, here, rows, rsem, slot):
        v = v[:, :KP] + mm(v[:, KP:KE].astype(BF), back[:, mycols])
        for j in range(7):
            gota[pl.ds(j, G, stride=8), :] = v[:, j * 256 : j * 256 + 128]
            gotb[pl.ds(j, G, stride=8), :] = v[:, j * 256 + 128 : (j + 1) * 256]
        msg[g * 8 : (g + 1) * 8, :, 0:128] = gota[...].astype(BF).reshape(8, G, 128)
        msg[g * 8 : (g + 1) * 8, :, 128:256] = gotb[...].astype(BF).reshape(8, G, 128)
        for dy in (2, 1, 3, 0):
            for cc in range(2):
                send(
                    msg.at[g * 8 + yp[dy] * 2 + cc], rows.at[slot, y], 16, rsem, fid(xx, zz, cc), yp[dy],
                    own=jnp.logical_and(c == cc, here) if dy == 0 else None,
                )

    def out0(ts):
        for t in ts:
            wait(hall.at[pl.ds(lax.div(t, 4) * 4, 4), m4(t)], hallr.at[t])

        def rows(kb):
            return jnp.concatenate(
                [hall[lax.div(t, 4) * 4 + m4(t + xx), m4(t), kb] for t in ts for xx in range(NX)], axis=0
            )

        def body(nb, carry):
            cols = pl.ds(pl.multiple_of(nb * NB, 128), NB)
            po[0 : 64 * len(ts), cols] = mm(rows(0), wd[0, :, cols]) + mm(rows(1), wd[1, :, cols])
            return carry

        lax.fori_loop(0, KE // NB, body, 0)

    def scatter0():
        right, left = fid(x, zr, 0), fid(x, zl, 0)
        out0([zf])
        for xx in range(2):
            ring(0, xx, po[xx * G : (xx + 1) * G, :], fid(x, zp[2], 0))
            ring(1, xx + 2, po[(xx + 2) * G : (xx + 3) * G, :], fid(x, zp[6], 0))
        for s in range(1, 4):
            out0([zp[4 - s], zp[4 + s]])
            for xx in range(NX):
                for d, tgt in ((0, right), (1, left)):
                    v = po[(4 * d + xx) * G : (4 * d + xx + 1) * G, :]
                    if s > 1:
                        v = v + come(d, (s - 1) * 4 + xx)
                    if s == 2 and xx // 2 == d:
                        v = v + come(d, xx)
                    ring(d, s * 4 + xx, v, tgt)
            (small_b, small_c, small_d)[s - 1]()
        out0([z])
        pl.semaphore_wait(zsem, NZ - 1)
        order_ext()
        for b in range(2):
            dlp[b] = mm_tn(extp[...], hall[:, :, b].reshape(512, H))[0:R]
        send(dlp.at[1], dlr.at[0], 15, lar.at[0], sib, y)
        for xx in range(NX):
            v = po[xx * G : (xx + 1) * G, :] + come(0, 12 + xx) + come(1, 12 + xx)
            last(xx, v, dlv, xx, z, x == xx, rows0, rowss.at[0], x)
        pl.when(x == y)(small_e)

    def out1(t, dst):
        wait(gall.at[:, 0], hallr.at[t])

        def rows(b):
            return jnp.concatenate(
                [gall[(zz // 4) * 4 + m4(t + zz), zz % 4, b] for zz in range(NZ)], axis=0
            )

        def body(nb, carry):
            cols = pl.ds(pl.multiple_of(nb * NB, 128), NB)
            acc = mm_nt(rows(0), wgu[0, cols, :])
            for b in range(1, 4):
                acc += mm_nt(rows(b), wgu[b, cols, :])
            dst[:, cols] = acc
            return carry

        lax.fori_loop(0, KE // NB, body, 0)

    def scatter1():
        right, left = fid(xrt, z, 1), fid(xlt, z, 1)
        out1(xf, po)
        for zz in range(4):
            ring(0, zz, po[zz * G : (zz + 1) * G, :], right)
            ring(1, zz + 4, po[(zz + 4) * G : (zz + 5) * G, :], left)
        out1(xrt, po)
        for zz in range(4, 8):
            ring(0, 8 + zz, po[zz * G : (zz + 1) * G, :], right)
        out1(xlt, pq)
        for zz in range(4):
            ring(1, 8 + zz, pq[zz * G : (zz + 1) * G, :], left)
        for zz in range(4):
            ring(0, 8 + zz, po[zz * G : (zz + 1) * G, :] + come(0, zz), right)
            ring(1, 12 + zz, pq[(zz + 4) * G : (zz + 5) * G, :] + come(1, zz + 4), left)
        small_b()
        out1(x, po)
        pl.semaphore_wait(zsem, NZ - 1)
        small_c()
        for i, zz in enumerate((0, 4, 1, 5, 2, 6, 3, 7)):
            v = po[zz * G : (zz + 1) * G, :] + come(0, 8 + zz) + come(1, 8 + zz)
            last(zz, v, gev, x, zz, z == zz, rows1, rowss.at[1], z)
            if i == 3:
                small_d()
        order_ext()
        for b in range(4):
            grad = mm_tn(extp[...], gall[:, :, b].reshape(512, H))
            dlp[b] = grad[0:R] if b < 2 else grad[R:EX]
        send(dlp.at[0], dlr.at[0], 15, lar.at[0], sib, y)
        send(dlp.at[2], dlr.at[1], 15, lar.at[1], sib, y)
        pl.when(x == y)(small_e)

    pl.when(c == 0)(scatter0)
    pl.when(c == 1)(scatter1)

    def give(pairs):
        for i, (ref, sem) in enumerate(pairs):
            if sem is not None:
                wait(ref, sem)
            pltpu.make_async_copy(ref, dla_out.at[i], outsem.at[i]).start()

    pl.when(c == 0)(lambda: give(((dlp.at[0], None), (dlr.at[0], lar.at[0]), (dlr.at[1], lar.at[1]))))
    pl.when(c == 1)(lambda: give(((dlr.at[0], lar.at[0]), (dlp.at[1], None), (dlp.at[3], None))))
    wait(fd.at[0], t3r.at[0])
    wait(fd.at[1], t3r.at[1])
    out_fd = pltpu.make_async_copy(fd, fd_out, outsem.at[3])
    out_fd.start()
    for kind, (rows, n) in enumerate(((rows0, NX), (rows1, NZ))):
        wait(rows, rowss.at[kind])
        v = rows[0].astype(F32)
        for i in range(1, n):
            v += rows[i].astype(F32)
        rowsf[kind] = v
        pltpu.make_async_copy(rowsf.at[kind], rows_out.at[kind], outsem.at[4 + kind]).start()
    sent(0, msg.at[pl.ds(0, 19)])

    @pl.when(c == 0)
    def _():
        sent(4, rsr.at[pl.ds(0, 28)])
        sent(6, part.at[pl.ds(0, 7)])
        sent(7, part.at[pl.ds(0, 4)])
        sent(8, part.at[pl.ds(0, 3), pl.ds(0, 2)])
        sent(14, rsr.at[pl.ds(0, 28)])
        sent(15, dlp.at[0])
        sent(16, msg.at[pl.ds(0, 31)])
        pl.when(x == y)(lambda: sent(17, part.at[pl.ds(0, 7), 0]))

    @pl.when(c == 1)
    def _():
        sent(4, rsr.at[pl.ds(0, 31)])
        sent(6, part.at[pl.ds(0, 7), pl.ds(0, 2)])
        sent(7, part.at[pl.ds(0, 3)])
        sent(8, part.at[pl.ds(0, 2)])
        sent(14, rsr.at[pl.ds(0, 24)])
        sent(15, dlp.at[pl.ds(0, 2)])
        sent(16, msg.at[pl.ds(0, 63)])
        pl.when(x == y)(lambda: sent(17, part.at[pl.ds(0, 7), 0]))

    sent(1, wgu.at[0])
    sent(2, wgu.at[0])
    sent(3, wd.at[0])
    sent(5, ext)
    sent(9, msg.at[pl.ds(0, 3)])
    sent(10, msg.at[pl.ds(0, 7)])
    sent(11, msg.at[pl.ds(0, 3)])
    for cc in range(2):
        @pl.when(jnp.logical_not(jnp.logical_and(c == cc, y == x)))
        def _(cc=cc):
            sent(12 + cc, smm.at[0])
    for i in range(3):
        wait(dlp.at[0], outsem.at[i])
    out_fd.wait()
    for kind in range(2):
        wait(rowsf.at[kind], outsem.at[4 + kind])


def place(rows_ref, fd_ref, dla_ref, lo, gt, dget, dgl, duet, dul, ddet, ddl, row):
    for kind, ref in enumerate((lo, gt)):
        for yy in range(NY):
            for t in range(2):
                for j in range(7):
                    row[t : t + 1, yy * KP + j * 256 : yy * KP + (j + 1) * 256] = rows_ref[
                        kind, yy, t * 8 + j : t * 8 + j + 1, :
                    ]
        ref[...] = row[...].astype(BF)
    v = fd_ref[0].astype(F32).T
    dget[...] = v[:R, :112]
    duet[...] = v[R:EX, :112]
    ddl[...] = fd_ref[1].astype(F32).T[:R, :112]
    ddet[...] = dla_ref[0]
    dgl[...] = dla_ref[1]
    dul[...] = dla_ref[2]


def dma(*shape):
    return pltpu.SemaphoreType.DMA(shape)


def on_device(
    tokens, grad_out, gate_codes, gate_scales, up_codes, up_scales, down_codes, down_scales,
    gate_enter, gate_leave, up_enter, up_leave, down_enter, down_leave,
):
    vm = pl.BlockSpec(memory_space=pltpu.VMEM)
    hb = pl.BlockSpec(memory_space=pltpu.HBM)
    V = pltpu.VMEM
    one = pltpu.SemaphoreType.DMA
    scratch = [
        V((2, NY * KP), BF), V((2, NY * KP), BF), V((3, 2, 14), BF), V((R, H), BF),
        V((KP, H), BF), V((KP, H), BF), V((H, KP), BF), V((EX, NY * KP), BF), V((EX, NY * KP), BF), dma(14),
        pltpu.SemaphoreType.REGULAR,
        V((2, NY, G, H), F32), V((2, NY, G, H), BF), V((NX, 8, G, H), BF), dma(NX),
        V((4, KE, H), BF), V((2, H, KE), BF), dma(3),
        V((NZ, NX, G, KE), BF), dma(32),
        V((NZ, NX, G, EX), BF), V((512, EX), BF), one,
        V((NZ, NX, 4, G, H), BF), V((NY, 4, 4, G, H), BF), dma(4),
        V((NX, NZ, 2, G, H), BF), V((NY, 4, 2, G, H), BF), dma(4),
        V((4, 2, G, H), BF), V((8, 4, 2, G, H), BF), dma(8),
        V((4, 4, G, H), BF), V((8, 4, 4, G, H), BF),
        V((128, KE), F32), V((128, KE), F32), V((32, G, KE), BF), V((32, G, KE), BF), dma(32),
        V((64, G, H), BF), V((NX, NY, G, H), BF), V((NZ, NY, G, H), BF), dma(2),
        V((2, NY, G, H), F32), dma(6), V((128, 128), F32), V((128, 128), F32),
        V((4, G, H), BF), V((NX, G, H), BF), one, V((G, H), BF), V((NZ, G, H), BF), one,
        V((G, H), BF), V((NX, G, H), BF), one, V((8, 4, G, EX), BF), one,
        V((384, EX), F32), V((2, EX, EX), BF), V((2, EX, EX), BF), dma(2),
        V((4, R, H), F32), V((2, R, H), F32), dma(2),
        dma(18),
    ]
    S = jax.ShapeDtypeStruct
    rows, fd, dla = pl.pallas_call(
        kernel,
        out_shape=[S((2, NY, G, H), F32), S((2, EX, EX), BF), S((3, R, H), F32)],
        in_specs=[hb] * 14,
        out_specs=[hb] * 3,
        scratch_shapes=scratch,
        compiler_params=pltpu.CompilerParams(
            collective_id=0, has_side_effects=True, vmem_limit_bytes=63 * 1024 * 1024
        ),
        name="lora_ffn_step",
    )(
        tokens, grad_out, gate_scales.T, up_scales.T, down_scales, gate_codes, up_codes, down_codes, gate_leave, up_leave, down_enter.T,
        gate_enter.T, up_enter.T, down_leave,
    )
    lo, gt, dget, dgl, duet, dul, ddet, ddl = pl.pallas_call(
        place,
        out_shape=[
            S((2, NY * KP), BF), S((2, NY * KP), BF), S((R, 112), F32), S((R, H), F32),
            S((R, 112), F32), S((R, H), F32), S((R, H), F32), S((R, 112), F32),
        ],
        in_specs=[vm] * 3,
        out_specs=[vm] * 8,
        scratch_shapes=[V((2, NY * KP), F32)],
        name="place_outputs",
    )(rows, fd, dla)
    return lo, gt, dget.T, dgl, duet.T, dul, ddet.T, ddl


def solution(mesh):
    return jax.shard_map(
        on_device,
        mesh=mesh,
        in_specs=(
            P(("fsdp", "dp"), None),
            P(("fsdp", "dp"), None),
            P("dp", "fsdp"),
            P("dp", "fsdp"),
            P("dp", "fsdp"),
            P("dp", "fsdp"),
            P("fsdp", "dp"),
            P("fsdp", "dp"),
            P(),
            P(None, "fsdp"),
            P(),
            P(None, "fsdp"),
            P("fsdp", None),
            P(),
        ),
        out_specs=(
            P(("fsdp", "dp"), None),
            P(("fsdp", "dp"), None),
            P("fsdp", None),
            P(None, "fsdp"),
            P("fsdp", None),
            P(None, "fsdp"),
            P("fsdp", None),
            P(None, "fsdp"),
        ),
        check_vma=False,
    )
```

```python
import jax
import jax.numpy as jnp
from jax import lax
from jax.experimental import pallas as pl
from jax.experimental.pallas import tpu as pltpu
from jax.sharding import PartitionSpec as P

NX, NZ, NY = 4, 8, 4
KP, KE, EX = 1792, 1920, 128
G, H, R = 16, 256, 64
NB = 384
BF, F32 = jnp.bfloat16, jnp.float32
MESH = pl.DeviceIdType.MESH


def mm(a, b):
    return jnp.dot(a, b, preferred_element_type=F32)


def mm_nt(a, b):
    return lax.dot_general(a, b, (((1,), (1,)), ((), ())), preferred_element_type=F32)


def mm_tn(a, b):
    return lax.dot_general(a, b, (((0,), (0,)), ((), ())), preferred_element_type=F32)


def kernel(
    tok_hbm, gout_hbm, gs_hbm, us_hbm, ds_hbm, gc_hbm, uc_hbm, dc_hbm, gl_hbm, ul_hbm, det_hbm, get_hbm, uet_hbm, dl_hbm,
    rows_out, fd_out, dla_out,
    tokv, goutv, scv, detv, gcv, ucv, dcv, gev, dlv, ldsem, zsem,
    sf, sends, st1, s1r,
    wgu, wd, wsr,
    aa, agr,
    ext, extp, exr,
    part, rgu, gur,
    parth, rh, hr,
    hb, hall, hallr,
    gb, gall,
    po, pq, rss, rsr, rsrs,
    msg, rows0, rows1, rowss, rowsf, outsem, gota, gotb,
    sp, sa, sar, sb, sc8, sc8r, sd, se, ser, smm, smr,
    res, mb, fd, t3r,
    dlp, dlr, lar,
    gsem,
):
    f = lax.axis_index("fsdp")
    y = lax.axis_index("dp")
    x = lax.div(f, 16)
    z = lax.rem(lax.div(f, 2), 8)
    c = lax.rem(f, 2)
    o = 1 - c

    def fid(xx, zz, cc):
        return xx * 16 + zz * 2 + cc

    def m4(v):
        return lax.rem(v, 4)

    def m8(v):
        return lax.rem(v, 8)

    zp = [m8(z + k) for k in range(NZ)]
    xp = [m4(x + k) for k in range(NX)]
    yp = [m4(y + k) for k in range(NY)]

    def rcopy(src, dst, ssem, rsem, ff, yy):
        return pltpu.make_async_remote_copy(
            src_ref=src, dst_ref=dst, send_sem=ssem, recv_sem=rsem,
            device_id={"fsdp": ff, "dp": yy}, device_id_type=MESH,
        )

    def wait(ref, sem):
        pltpu.make_async_copy(ref, ref, sem).wait()

    def send(src, dst, kind, rsem, ff, yy, own=None):
        ssem = gsem.at[kind]
        if own is None:
            rcopy(src, dst, ssem, rsem, ff, yy).start()
            return

        @pl.when(own)
        def _():
            pltpu.make_async_copy(src, dst, rsem).start()

        @pl.when(jnp.logical_not(own))
        def _():
            rcopy(src, dst, ssem, rsem, ff, yy).start()

    def sent(kind, ref):
        wait(ref, gsem.at[kind])

    loads = [
        pltpu.make_async_copy(get_hbm, gev.at[pl.ds(0, R)], ldsem.at[0]),
        pltpu.make_async_copy(uet_hbm, gev.at[pl.ds(R, R)], ldsem.at[1]),
        pltpu.make_async_copy(dl_hbm, dlv.at[pl.ds(0, R)], ldsem.at[2]),
        pltpu.make_async_copy(gc_hbm, gcv, ldsem.at[3]),
        pltpu.make_async_copy(uc_hbm, ucv, ldsem.at[4]),
        pltpu.make_async_copy(dc_hbm, dcv, ldsem.at[5]),
        pltpu.make_async_copy(tok_hbm, tokv, ldsem.at[6]),
        pltpu.make_async_copy(gout_hbm, goutv, ldsem.at[7]),
        pltpu.make_async_copy(gs_hbm, scv.at[0], ldsem.at[8]),
        pltpu.make_async_copy(gl_hbm, wgu.at[c, pl.ds(KP, R)], ldsem.at[9]),
        pltpu.make_async_copy(ul_hbm, wgu.at[2 + c, pl.ds(KP + R, R)], ldsem.at[10]),
        pltpu.make_async_copy(det_hbm, detv, ldsem.at[11]),
        pltpu.make_async_copy(us_hbm, scv.at[1], ldsem.at[12]),
        pltpu.make_async_copy(ds_hbm, scv.at[2], ldsem.at[13]),
    ]
    for i in (6, 7, 0, 1, 2, 8, 12, 13, 9, 3, 10, 4, 11, 5):
        loads[i].start()

    barrier = pltpu.get_barrier_semaphore()
    peers = []
    for dx in range(NX):
        for dy in range(NY):
            for dc in range(2):
                if dx or dy or dc:
                    peers.append((fid(xp[dx], z, lax.rem(c + dc, 2)), yp[dy]))
    for dz in range(1, NZ):
        peers.append((fid(x, zp[dz], c), y))
    for ff, yy in peers:
        pl.semaphore_signal(barrier, inc=1, device_id={"fsdp": ff, "dp": yy}, device_id_type=MESH)

    dlv[R:EX, :] = jnp.zeros((R, NY * KP), BF)
    for kind, ref in enumerate((tokv, goutv)):
        loads[6 + kind].wait()
        v = ref[...].astype(F32)
        v16 = jnp.concatenate([v, jnp.zeros((14, NY * KP), F32)], axis=0).astype(BF)
        for yy in range(NY):
            for t in range(2):
                for j in range(7):
                    sf[kind, yy, t * 8 + j : t * 8 + j + 1, :] = v[
                        t : t + 1, yy * KP + j * 256 : yy * KP + (j + 1) * 256
                    ]
        if kind == 0:
            loads[0].wait()
            loads[1].wait()
            e = mm_nt(v16, gev[...])
        else:
            loads[2].wait()
            e = mm_nt(v16, dlv[...])
        for yy in range(NY):
            for t in range(2):
                sf[kind, yy, t * 8 + 7 : t * 8 + 8, :] = jnp.concatenate(
                    [e[t : t + 1], jnp.zeros((1, EX), F32)], axis=1
                )
    sends[...] = sf[...].astype(BF)
    pl.semaphore_wait(barrier, len(peers))

    for dz in range(1, NZ):
        pl.semaphore_signal(
            zsem, inc=1, device_id={"fsdp": fid(x, zp[dz], c), "dp": y}, device_id_type=MESH
        )

    src1 = y * 2 + c
    for dy in (2, 1, 3, 0):
        send(
            sends.at[1, yp[dy]], st1.at[x, src1], 0, s1r.at[x], fid(x, z, 1), yp[dy],
            own=(c == 1) if dy == 0 else None,
        )
    for dx in (0, 1, 3, 2):
        for dy in (2, 1, 3, 0):
            send(
                sends.at[0, yp[dy]], st1.at[x, src1], 0, s1r.at[x], fid(xp[dx], z, 0), yp[dy],
                own=(c == 0) if dx == 0 and dy == 0 else None,
            )

    def scale(k, i):
        lane = lax.broadcasted_iota(jnp.int32, (2, 14), 1)
        return jnp.sum(jnp.where(lane == i, scv[k].astype(F32), 0.0), axis=1, keepdims=True)

    def dequant_cols(codes, slot, k):
        def body(i, carry):
            rows = pl.ds(pl.multiple_of(i * 128, 128), 128)
            v = scale(k, i)
            wgu[slot, rows, 0:128] = (codes[rows, 0:128].astype(F32) * v[0:1]).astype(BF)
            wgu[slot, rows, 128:256] = (codes[rows, 128:256].astype(F32) * v[1:2]).astype(BF)
            return carry

        lax.fori_loop(0, 14, body, 0)

    sib = fid(x, z, o)
    for i in (8, 12, 13):
        loads[i].wait()
    loads[3].wait()
    dequant_cols(gcv, c, 0)
    loads[9].wait()
    wgu[c, KP + R :, :] = jnp.zeros((R, H), BF)
    send(wgu.at[c], wgu.at[c], 1, wsr.at[0], sib, y)
    loads[4].wait()
    dequant_cols(ucv, 2 + c, 1)
    wgu[2 + c, KP : KP + R, :] = jnp.zeros((R, H), BF)
    loads[10].wait()
    send(wgu.at[2 + c], wgu.at[2 + c], 2, wsr.at[1], sib, y)
    loads[5].wait()
    loads[11].wait()

    def dequant_down(i, carry):
        cols = pl.ds(pl.multiple_of(i * 128, 128), 128)
        v = scale(2, i)
        wd[c, 0:128, cols] = (dcv[0:128, cols].astype(F32) * v[0:1]).astype(BF)
        wd[c, 128:256, cols] = (dcv[128:256, cols].astype(F32) * v[1:2]).astype(BF)
        return carry

    lax.fori_loop(0, 14, dequant_down, 0)
    det = jnp.concatenate([detv[...].astype(F32), jnp.zeros((R, H), F32)], axis=0)
    wd[c, :, KP:KE] = det.T.astype(BF)
    send(wd.at[c], wd.at[c], 3, wsr.at[2], sib, y)

    def unpack(xx):
        wait(st1.at[xx], s1r.at[xx])
        got = st1[xx].reshape(128, H).astype(F32)
        for h, part_ref in enumerate((gota, gotb)):
            part_ref[0:128, :] = got[:, h * 128 : (h + 1) * 128]
            for j in range(8 - h):
                k = 2 * j + h
                aa[z, xx, :, k * 128 : (k + 1) * 128] = part_ref[pl.ds(j, G, stride=8), :].astype(BF)

    flag = jnp.where(y == 0, 1.0, 0.0).astype(F32)

    def masked(v):
        return (v.astype(F32) * flag).astype(BF)

    def have(zz, xx):
        wait(aa.at[zz, xx], agr.at[zz * 4 + xx])

    def fwd(zz, xx, tz, tx):
        send(aa.at[zz, xx], aa.at[zz, xx], 4, agr.at[zz * 4 + xx], fid(tx, tz, c), y)

    zr, zl, zf = zp[1], zp[7], zp[4]
    xrt, xlt, xf = xp[1], xp[3], xp[2]

    def weights():
        wait(wgu.at[o], wsr.at[0])
        wait(wgu.at[2 + o], wsr.at[1])
        wait(wd.at[o], wsr.at[2])

    def front0(zs):
        def body(b, carry):
            a = jnp.concatenate([aa[zz].reshape(64, KE) for zz in zs], axis=0)
            acc = mm(a[:, :KP], wgu[b, 0:KP, :]) + mm(masked(a[:, KP:]), wgu[b, KP:KE, :])
            acc = acc.astype(BF)
            for i, zz in enumerate(zs):
                part[zz, :, b] = acc[i * 64 : (i + 1) * 64].reshape(4, G, H)
            return carry

        lax.fori_loop(0, 4, body, 0)
        for zz in zs:
            for xx in range(NX):
                send(
                    part.at[zz, xx], rgu.at[y, m4(zz)], 6, gur.at[m4(zz)],
                    fid(x, z, lax.div(zz, 4)), m4(zz + xx),
                    own=jnp.logical_and(m4(zz + xx) == y, zz < 4),
                )

    def front1(xx):
        def body(b, carry):
            a = aa[:, xx].reshape(128, KE)
            acc = mm_nt(a[:, :KP], wd[b, :, 0:KP]) + mm_nt(masked(a[:, KP:]), wd[b, :, KP:KE])
            parth[xx, :, b] = acc.astype(BF).reshape(8, G, H)
            return carry

        lax.fori_loop(0, 2, body, 0)
        for zz in range(NZ):
            send(
                parth.at[xx, zz], rh.at[y, zz % 4], 6, hr.at[zz % 4],
                fid(x, z, zz // 4), m4(xx + zz), own=(m4(xx + zz) == y) if zz >= 4 else None,
            )

    def gather0():
        for xx in (x, xrt, xlt, xf):
            unpack(xx)
            fwd(z, xx, zr, x)
            fwd(z, xx, zl, x)
        weights()
        front0([z])
        for k in range(1, 4):
            za, zb = zp[8 - k], zp[k]
            for i, xx in enumerate((x, xrt, xlt, xf)):
                have(za, xx)
                if k < 3:
                    fwd(za, xx, zr, x)
                if k == 2 and i < 2:
                    fwd(za, xx, zp[2], x)
                have(zb, xx)
                if k < 3:
                    fwd(zb, xx, zl, x)
                if k == 2 and i >= 2:
                    fwd(zb, xx, zp[6], x)
            front0([za, zb])
        for xx in range(NX):
            have(zf, xx)
        send(aa.at[:, :, :, pl.ds(KP, EX)], ext, 5, exr, sib, y)
        front0([zf])

    def gather1():
        unpack(x)
        for dz in (1, 7, 2, 6):
            fwd(z, x, zp[dz], x)

        def spread(zz, far=False):
            fwd(zz, x, z, xrt)
            fwd(zz, x, z, xlt)
            if far:
                fwd(zz, x, z, xf)

        def xstep(dz, up=False):
            a, b = (xlt, xrt) if up else (xrt, xlt)
            have(zp[dz], a)
            fwd(zp[dz], a, z, b)

        spread(z)
        have(zp[7], x)
        spread(zp[7])
        have(zp[1], x)
        spread(zp[1])
        have(zp[6], x)
        fwd(zp[6], x, zr, x)
        fwd(zp[6], x, zp[2], x)
        have(zp[2], x)
        fwd(zp[2], x, zl, x)
        spread(zp[6])
        spread(zp[2])
        xstep(0, True)
        xstep(7)
        xstep(1, True)
        have(zp[4], x)
        spread(zp[4], True)
        for dz in (5, 3):
            have(zp[dz], x)
            spread(zp[dz])
        xstep(6)
        xstep(2)
        weights()
        front1(x)
        xstep(5, True)
        xstep(3)
        for dz in (0, 1, 4, 5):
            have(zp[dz], xrt)
        front1(xrt)
        for dz in (7, 6, 2, 3, 4):
            have(zp[dz], xlt)
        front1(xlt)
        for dz in range(NZ):
            have(zp[dz], xf)
        send(aa.at[:, :, :, pl.ds(KP, EX)], ext, 5, exr, sib, y)
        front1(xf)

    pl.when(c == 0)(gather0)
    pl.when(c == 1)(gather1)

    def middle(q, carry):
        wait(rgu.at[:, q], gur.at[q])
        wait(rh.at[:, q], hr.at[q])
        for b in range(2):
            g = rgu[0, q, b].astype(F32)
            u = rgu[0, q, 2 + b].astype(F32)
            h = rh[0, q, b].astype(F32)
            for s in range(1, NY):
                g += rgu[s, q, b].astype(F32)
                u += rgu[s, q, 2 + b].astype(F32)
                h += rh[s, q, b].astype(F32)
            sig = jax.nn.sigmoid(g)
            act = g * sig
            hb[q, b] = (act * u).astype(BF)
            gb[q, b] = (h * u * sig * (1.0 + g * (1.0 - sig))).astype(BF)
            gb[q, 2 + b] = (h * act).astype(BF)
        return carry

    lax.fori_loop(0, 4, middle, 0)
    blk = c * 4 + y
    def give_hidden(i):
        qh = m4(z + (0, 3, 1, 2)[i])
        for dy in (2, 1, 3, 0):
            send(hb.at[qh], hall.at[blk, qh], 8, hallr.at[c * 4 + qh], fid(x, z, 0), yp[dy],
                 own=(c == 0) if dy == 0 else None)

    def give_grads(i):
        qg = m4(y + 8 - x - (2, 1, 3, 0)[i])
        for dy in (2, 1, 3, 0):
            send(gb.at[qg], gall.at[blk, qg], 7, hallr.at[m4(y + 4 - qg)], fid(x, z, 1), yp[dy],
                 own=(c == 1) if dy == 0 else None)

    for fn, i in (
        (give_hidden, 0), (give_hidden, 1), (give_hidden, 2), (give_grads, 0), (give_grads, 1), (give_grads, 2), (give_hidden, 3), (give_grads, 3),
    ):
        fn(i)

    def small_a():
        mids = jnp.zeros((64, EX), F32)
        backs = jnp.zeros((64, EX), F32)
        for b in range(2):
            mids += mm(hb[:, b].reshape(64, H), wd[b, :, KP:KE])
        for b in range(4):
            backs += mm_nt(gb[:, b].reshape(64, H), wgu[b, KP:KE, :])
        sp[:, :, 0:EX] = mids.astype(BF).reshape(4, G, EX)
        sp[:, :, EX : 2 * EX] = backs.astype(BF).reshape(4, G, EX)
        for q in range(NX):
            send(sp.at[q], sa.at[x], 9, sar, fid(q, z, c), y, own=x == q)

    small_a()

    def small_b():
        wait(sa, sar)
        v = sa[0].astype(F32)
        for i in range(1, NX):
            v += sa[i].astype(F32)
        sb[...] = v.astype(BF)
        for dz in (4, 3, 5, 2, 6, 1, 7):
            send(sb, sc8.at[z], 10, sc8r, fid(x, zp[dz], c), y)

    def small_c():
        v = sb[...].astype(F32)
        wait(sc8.at[pl.ds(0, NZ - 1)], sc8r)
        for dz in range(1, NZ):
            v += sc8[zp[dz]].astype(F32)
        sd[...] = v.astype(BF)
        for dx in (2, 1, 3):
            send(sd, se.at[x], 11, ser, fid(xp[dx], z, c), y)

    def small_d():
        wait(se.at[pl.ds(0, NX - 1)], ser)
        se[x] = sd[...]
        for cc in range(2):
            lanes = pl.ds((1 - cc) * EX, EX)
            send(se.at[:, :, lanes], smm.at[blk], 12 + cc, smr, fid(x, z, cc), x,
                 own=jnp.logical_and(c == cc, y == x))

    def small_e():
        wait(smm, smr)
        small = jnp.concatenate(
            [smm[(zz // 4) * 4 + (xx + zz) % 4, zz % 4] for zz in range(NZ) for xx in range(NX)], axis=0
        )
        first = lax.div(z * 224, 128) * 128
        lead = z * 224 - first
        win = pl.ds(pl.multiple_of(first, 128), 384)
        res[...] = mm_tn(aa[:, :, :, win].reshape(512, 384), small)
        for cc in range(2):
            mb[cc, 0:112, :] = res[pl.ds(pl.multiple_of(lead + cc * 112, 8), 112), :].astype(BF)
        for dy in (2, 1, 3, 0):
            for cc in range(2):
                send(
                    mb.at[cc], fd.at[c], 17, t3r.at[c], fid(x, z, cc), yp[dy],
                    own=(c == cc) if dy == 0 else None,
                )

    def order_ext():
        wait(ext, exr)
        for i in range(8):
            for q in range(4):
                zz = (i // 4) * 4 + q
                extp[(i * 4 + q) * G : (i * 4 + q + 1) * G, :] = ext[zz, (i % 4 + 8 - zz) % 4]

    def ring(d, slot, v, tgt):
        k = d * 16 + slot
        rss[k] = v.astype(BF)
        send(rss.at[k], rsr.at[k], 14, rsrs.at[k], tgt, y)

    def come(d, slot):
        k = d * 16 + slot
        wait(rsr.at[k], rsrs.at[k])
        return rsr[k].astype(F32)

    mycols = pl.ds(pl.multiple_of(y * KP, 128), KP)

    def last(g, v, back, xx, zz, here, rows, rsem, slot):
        v = v[:, :KP] + mm(v[:, KP:KE].astype(BF), back[:, mycols])
        for j in range(7):
            gota[pl.ds(j, G, stride=8), :] = v[:, j * 256 : j * 256 + 128]
            gotb[pl.ds(j, G, stride=8), :] = v[:, j * 256 + 128 : (j + 1) * 256]
        msg[g * 8 : (g + 1) * 8, :, 0:128] = gota[0:128, :].astype(BF).reshape(8, G, 128)
        msg[g * 8 : (g + 1) * 8, :, 128:256] = gotb[0:128, :].astype(BF).reshape(8, G, 128)
        for dy in (2, 1, 3, 0):
            for cc in range(2):
                send(
                    msg.at[g * 8 + yp[dy] * 2 + cc], rows.at[slot, y], 16, rsem, fid(xx, zz, cc), yp[dy],
                    own=jnp.logical_and(c == cc, here) if dy == 0 else None,
                )

    def out0(ts):
        for t in ts:
            wait(hall.at[pl.ds(lax.div(t, 4) * 4, 4), m4(t)], hallr.at[t])

        def rows(kb):
            return jnp.concatenate(
                [hall[lax.div(t, 4) * 4 + m4(t + xx), m4(t), kb] for t in ts for xx in range(NX)], axis=0
            )

        def body(nb, carry):
            cols = pl.ds(pl.multiple_of(nb * NB, 128), NB)
            po[0 : 64 * len(ts), cols] = mm(rows(0), wd[0, :, cols]) + mm(rows(1), wd[1, :, cols])
            return carry

        lax.fori_loop(0, KE // NB, body, 0)

    def scatter0():
        right, left = fid(x, zr, 0), fid(x, zl, 0)
        out0([zf])
        for xx in range(2):
            ring(0, xx, po[xx * G : (xx + 1) * G, :], fid(x, zp[2], 0))
            ring(1, xx + 2, po[(xx + 2) * G : (xx + 3) * G, :], fid(x, zp[6], 0))
        for s in range(1, 4):
            out0([zp[4 - s], zp[4 + s]])
            for xx in range(NX):
                for d, tgt in ((0, right), (1, left)):
                    v = po[(4 * d + xx) * G : (4 * d + xx + 1) * G, :]
                    if s > 1:
                        v = v + come(d, (s - 1) * 4 + xx)
                    if s == 2 and xx // 2 == d:
                        v = v + come(d, xx)
                    ring(d, s * 4 + xx, v, tgt)
            (small_b, small_c, small_d)[s - 1]()
        out0([z])
        pl.semaphore_wait(zsem, NZ - 1)
        order_ext()
        for b in range(2):
            dlp[b] = mm_tn(extp[...], hall[:, :, b].reshape(512, H))[0:R]
        send(dlp.at[1], dlr.at[0], 15, lar.at[0], sib, y)
        for xx in range(NX):
            v = po[xx * G : (xx + 1) * G, :] + come(0, 12 + xx) + come(1, 12 + xx)
            last(xx, v, dlv, xx, z, x == xx, rows0, rowss.at[0], x)
        pl.when(x == y)(small_e)

    def out1(t, dst):
        wait(gall.at[:, 0], hallr.at[t])

        def rows(b):
            return jnp.concatenate(
                [gall[(zz // 4) * 4 + m4(t + zz), zz % 4, b] for zz in range(NZ)], axis=0
            )

        def body(nb, carry):
            cols = pl.ds(pl.multiple_of(nb * NB, 128), NB)
            acc = mm_nt(rows(0), wgu[0, cols, :])
            for b in range(1, 4):
                acc += mm_nt(rows(b), wgu[b, cols, :])
            dst[:, cols] = acc
            return carry

        lax.fori_loop(0, KE // NB, body, 0)

    def scatter1():
        right, left = fid(xrt, z, 1), fid(xlt, z, 1)
        out1(xf, po)
        for zz in range(4):
            ring(0, zz, po[zz * G : (zz + 1) * G, :], right)
            ring(1, zz + 4, po[(zz + 4) * G : (zz + 5) * G, :], left)
        out1(xrt, po)
        for zz in range(4, 8):
            ring(0, 8 + zz, po[zz * G : (zz + 1) * G, :], right)
        out1(xlt, pq)
        for zz in range(4):
            ring(1, 8 + zz, pq[zz * G : (zz + 1) * G, :], left)
        for zz in range(4):
            ring(0, 8 + zz, po[zz * G : (zz + 1) * G, :] + come(0, zz), right)
            ring(1, 12 + zz, pq[(zz + 4) * G : (zz + 5) * G, :] + come(1, zz + 4), left)
        small_b()
        out1(x, po)
        pl.semaphore_wait(zsem, NZ - 1)
        small_c()
        for i, zz in enumerate((0, 4, 1, 5, 2, 6, 3, 7)):
            v = po[zz * G : (zz + 1) * G, :] + come(0, 8 + zz) + come(1, 8 + zz)
            last(zz, v, gev, x, zz, z == zz, rows1, rowss.at[1], z)
            if i == 3:
                small_d()
        order_ext()
        for b in range(4):
            grad = mm_tn(extp[...], gall[:, :, b].reshape(512, H))
            dlp[b] = grad[0:R] if b < 2 else grad[R:EX]
        send(dlp.at[0], dlr.at[0], 15, lar.at[0], sib, y)
        send(dlp.at[2], dlr.at[1], 15, lar.at[1], sib, y)
        pl.when(x == y)(small_e)

    pl.when(c == 0)(scatter0)
    pl.when(c == 1)(scatter1)

    def give(pairs):
        for i, (ref, sem) in enumerate(pairs):
            if sem is not None:
                wait(ref, sem)
            pltpu.make_async_copy(ref, dla_out.at[i], outsem.at[i]).start()

    pl.when(c == 0)(lambda: give(((dlp.at[0], None), (dlr.at[0], lar.at[0]), (dlr.at[1], lar.at[1]))))
    pl.when(c == 1)(lambda: give(((dlr.at[0], lar.at[0]), (dlp.at[1], None), (dlp.at[3], None))))
    wait(fd.at[0], t3r.at[0])
    wait(fd.at[1], t3r.at[1])
    out_fd = pltpu.make_async_copy(fd, fd_out, outsem.at[3])
    out_fd.start()
    for kind, (rows, n) in enumerate(((rows0, NX), (rows1, NZ))):
        wait(rows, rowss.at[kind])
        v = rows[0].astype(F32)
        for i in range(1, n):
            v += rows[i].astype(F32)
        rowsf[kind] = v
        pltpu.make_async_copy(rowsf.at[kind], rows_out.at[kind], outsem.at[4 + kind]).start()
    sent(0, msg.at[pl.ds(0, 19)])

    @pl.when(c == 0)
    def _():
        sent(4, rsr.at[pl.ds(0, 28)])
        sent(6, part.at[pl.ds(0, 7)])
        sent(7, part.at[pl.ds(0, 4)])
        sent(8, part.at[pl.ds(0, 3), pl.ds(0, 2)])
        sent(14, rsr.at[pl.ds(0, 28)])
        sent(15, dlp.at[0])
        sent(16, msg.at[pl.ds(0, 31)])
        pl.when(x == y)(lambda: sent(17, part.at[pl.ds(0, 7), 0]))

    @pl.when(c == 1)
    def _():
        sent(4, rsr.at[pl.ds(0, 31)])
        sent(6, part.at[pl.ds(0, 7), pl.ds(0, 2)])
        sent(7, part.at[pl.ds(0, 3)])
        sent(8, part.at[pl.ds(0, 2)])
        sent(14, rsr.at[pl.ds(0, 24)])
        sent(15, dlp.at[pl.ds(0, 2)])
        sent(16, msg.at[pl.ds(0, 63)])
        pl.when(x == y)(lambda: sent(17, part.at[pl.ds(0, 7), 0]))

    sent(1, wgu.at[0])
    sent(2, wgu.at[0])
    sent(3, wd.at[0])
    sent(5, ext)
    sent(9, msg.at[pl.ds(0, 3)])
    sent(10, msg.at[pl.ds(0, 7)])
    sent(11, msg.at[pl.ds(0, 3)])
    for cc in range(2):
        @pl.when(jnp.logical_not(jnp.logical_and(c == cc, y == x)))
        def _(cc=cc):
            sent(12 + cc, smm.at[0])
    for i in range(3):
        wait(dlp.at[0], outsem.at[i])
    out_fd.wait()
    for kind in range(2):
        wait(rowsf.at[kind], outsem.at[4 + kind])


def place(rows_ref, fd_ref, dla_ref, lo, gt, dget, dgl, duet, dul, ddet, ddl, row):
    for kind, ref in enumerate((lo, gt)):
        for yy in range(NY):
            for t in range(2):
                for j in range(7):
                    row[t : t + 1, yy * KP + j * 256 : yy * KP + (j + 1) * 256] = rows_ref[
                        kind, yy, t * 8 + j : t * 8 + j + 1, :
                    ]
        ref[...] = row[...].astype(BF)
    v = fd_ref[0].astype(F32).T
    dget[...] = v[:R, :112]
    duet[...] = v[R:EX, :112]
    ddl[...] = fd_ref[1].astype(F32).T[:R, :112]
    ddet[...] = dla_ref[0]
    dgl[...] = dla_ref[1]
    dul[...] = dla_ref[2]


def dma(*shape):
    return pltpu.SemaphoreType.DMA(shape)


def on_device(
    tokens, grad_out, gate_codes, gate_scales, up_codes, up_scales, down_codes, down_scales,
    gate_enter, gate_leave, up_enter, up_leave, down_enter, down_leave,
):
    vm = pl.BlockSpec(memory_space=pltpu.VMEM)
    hb = pl.BlockSpec(memory_space=pltpu.HBM)
    V = pltpu.VMEM
    one = pltpu.SemaphoreType.DMA
    scratch = [
        V((2, NY * KP), BF), V((2, NY * KP), BF), V((3, 2, 14), BF), V((R, H), BF),
        V((KP, H), BF), V((KP, H), BF), V((H, KP), BF), V((EX, NY * KP), BF), V((EX, NY * KP), BF), dma(14),
        pltpu.SemaphoreType.REGULAR,
        V((2, NY, G, H), F32), V((2, NY, G, H), BF), V((NX, 8, G, H), BF), dma(NX),
        V((4, KE, H), BF), V((2, H, KE), BF), dma(3),
        V((NZ, NX, G, KE), BF), dma(32),
        V((NZ, NX, G, EX), BF), V((512, EX), BF), one,
        V((NZ, NX, 4, G, H), BF), V((NY, 4, 4, G, H), BF), dma(4),
        V((NX, NZ, 2, G, H), BF), V((NY, 4, 2, G, H), BF), dma(4),
        V((4, 2, G, H), BF), V((8, 4, 2, G, H), BF), dma(8),
        V((4, 4, G, H), BF), V((8, 4, 4, G, H), BF),
        V((128, KE), F32), V((128, KE), F32), V((32, G, KE), BF), V((32, G, KE), BF), dma(32),
        V((64, G, H), BF), V((NX, NY, G, H), BF), V((NZ, NY, G, H), BF), dma(2),
        V((2, NY, G, H), F32), dma(6), V((136, 128), F32), V((136, 128), F32),
        V((4, G, H), BF), V((NX, G, H), BF), one, V((G, H), BF), V((NZ, G, H), BF), one,
        V((G, H), BF), V((NX, G, H), BF), one, V((8, 4, G, EX), BF), one,
        V((384, EX), F32), V((2, EX, EX), BF), V((2, EX, EX), BF), dma(2),
        V((4, R, H), F32), V((2, R, H), F32), dma(2),
        dma(18),
    ]
    S = jax.ShapeDtypeStruct
    rows, fd, dla = pl.pallas_call(
        kernel,
        out_shape=[S((2, NY, G, H), F32), S((2, EX, EX), BF), S((3, R, H), F32)],
        in_specs=[hb] * 14,
        out_specs=[hb] * 3,
        scratch_shapes=scratch,
        compiler_params=pltpu.CompilerParams(
            collective_id=0, has_side_effects=True, vmem_limit_bytes=63 * 1024 * 1024
        ),
        name="lora_ffn_step",
    )(
        tokens, grad_out, gate_scales.T, up_scales.T, down_scales, gate_codes, up_codes, down_codes, gate_leave, up_leave, down_enter.T,
        gate_enter.T, up_enter.T, down_leave,
    )
    lo, gt, dget, dgl, duet, dul, ddet, ddl = pl.pallas_call(
        place,
        out_shape=[
            S((2, NY * KP), BF), S((2, NY * KP), BF), S((R, 112), F32), S((R, H), F32),
            S((R, 112), F32), S((R, H), F32), S((R, H), F32), S((R, 112), F32),
        ],
        in_specs=[vm] * 3,
        out_specs=[vm] * 8,
        scratch_shapes=[V((2, NY * KP), F32)],
        name="place_outputs",
    )(rows, fd, dla)
    return lo, gt, dget.T, dgl, duet.T, dul, ddet.T, ddl


def solution(mesh):
    return jax.shard_map(
        on_device,
        mesh=mesh,
        in_specs=(
            P(("fsdp", "dp"), None),
            P(("fsdp", "dp"), None),
            P("dp", "fsdp"),
            P("dp", "fsdp"),
            P("dp", "fsdp"),
            P("dp", "fsdp"),
            P("fsdp", "dp"),
            P("fsdp", "dp"),
            P(),
            P(None, "fsdp"),
            P(),
            P(None, "fsdp"),
            P("fsdp", None),
            P(),
        ),
        out_specs=(
            P(("fsdp", "dp"), None),
            P(("fsdp", "dp"), None),
            P("fsdp", None),
            P(None, "fsdp"),
            P("fsdp", None),
            P(None, "fsdp"),
            P("fsdp", None),
            P(None, "fsdp"),
        ),
        check_vma=False,
    )
```
